32 devices in a mesh: cluster: 4 (over x, core), row: 8 (over z, y).
Axes of the slice: x: 2, y: 2, z: 4, core: 2. Of those that a mesh axis runs over, the one named last changes fastest.
Arguments:
- sources: bfloat16 [8192, 512], P(('cluster', 'row')), may hold values from -12 to 12
- targets: bfloat16 [8192, 512], P(('cluster', 'row')), may hold values from -12 to 12
- source_order: int32 [8192], P(('cluster', 'row')), may hold values from 0 to 255, as said below
- target_order: int32 [8192], P(('cluster', 'row')), may hold values from 0 to 255, as said below
Outputs:
- source_map: bfloat16 [8192, 512], P(('cluster', 'row'))
- target_map: bfloat16 [8192, 512], P(('cluster', 'row'))
The draws below stay inside these ranges and needn't reach their ends.
Inputs may be any that keep to these rules, and one draw needn't show every extreme that they name: `source_order`: in each aligned block of 256 consecutive rows every value appears exactly once, so each block holds 64 source rows of every co-cluster. `target_order`: in each aligned block of 256 consecutive rows every value appears exactly once, so each block holds 64 target rows of every co-cluster.
All inputs are finite; a program needn't handle non-finite values.
Results may differ from the reference program's by a relative error of at most 0.01.
Values may be sent and summed in bfloat16 or wider, within the bound.
A program may use at most 64 MiB of HBM per device.

```python
import math
import jax
import jax.numpy as jnp
from jax import lax

D = 512
ROWS_DEV = 256
ITERS = 3
CLUSTERS = 4
CPC = 2048
ROWS = 8192
PER = 64


def block_orders(key, salt):
    blocks = ROWS // ROWS_DEV
    subkeys = jax.random.split(jax.random.fold_in(key, salt), blocks)
    shuffled = jax.vmap(lambda subkey: jax.random.permutation(subkey, ROWS_DEV))(subkeys)
    return shuffled.reshape(-1).astype(jnp.int32)


def draw_source_order(key, part):
    return block_orders(key, 11)


def draw_target_order(key, part):
    return block_orders(key, 12)


def base_rows(key, salt):
    noise = jnp.clip(jax.random.normal(jax.random.fold_in(key, salt), (ROWS, D), jnp.float32), -5.0, 5.0)
    logs = jax.random.uniform(jax.random.fold_in(key, salt + 1), (ROWS, 1), jnp.float32, math.log(0.4), math.log(2.0))
    return noise * jnp.exp(logs)


def draw_sources(key, part):
    base = base_rows(key, 31)
    result = base
    return result.astype(jnp.bfloat16)


def draw_targets(key, part):
    base = base_rows(key, 41)
    result = base
    return result.astype(jnp.bfloat16)


def setup_inputs(seed: int = 0) -> dict:
    arg_keys = jax.random.split(jax.random.key(seed), 5)
    return {
        "sources": draw_sources(jax.random.fold_in(arg_keys[4], 71), 0),
        "targets": draw_targets(jax.random.fold_in(arg_keys[4], 71), 0),
        "source_order": draw_source_order(jax.random.fold_in(arg_keys[4], 71), 0),
        "target_order": draw_target_order(jax.random.fold_in(arg_keys[4], 71), 0),
    }


entropy_weight = 0.02


def square_sums(matrix):
    widened = matrix.astype(jnp.float32)
    return jnp.sum(widened * widened, axis=1)


def log_sum_exp(scores, axis):
    highest = jnp.max(scores, axis=axis, keepdims=True)
    return jnp.squeeze(highest, axis) + jnp.log(jnp.sum(jnp.exp(scores - highest), axis=axis))


def one_cluster(members):
    source_rows, target_rows = members
    inner = jnp.dot(source_rows, target_rows.T, preferred_element_type=jnp.float32)
    cost = (square_sums(source_rows)[:, None] + square_sums(target_rows)[None, :] - 2.0 * inner) / D
    log_mass = -math.log(CPC)
    target_potential = jnp.zeros((CPC,), jnp.float32)
    for repeat in range(ITERS):
        source_potential = entropy_weight * (log_mass - log_sum_exp((target_potential[None, :] - cost) / entropy_weight, 1))
        column_scores = (source_potential[:, None] - cost) / entropy_weight
        column_norm = log_sum_exp(column_scores, 0)
        target_potential = entropy_weight * (log_mass - column_norm)
    target_weight = jnp.exp(column_scores - column_norm[None, :]).astype(jnp.bfloat16)
    target_map = jnp.dot(target_weight.T, source_rows, preferred_element_type=jnp.float32).astype(jnp.bfloat16)
    row_scores = (target_potential[None, :] - cost) / entropy_weight
    row_norm = log_sum_exp(row_scores, 1)
    source_weight = jnp.exp(row_scores - row_norm[:, None]).astype(jnp.bfloat16)
    source_map = jnp.dot(source_weight, target_rows, preferred_element_type=jnp.float32).astype(jnp.bfloat16)
    return source_map, target_map


def reference(sources, targets, source_order, target_order):
    source_index = jnp.argsort(source_order // PER, stable=True).astype(jnp.int32).reshape(CLUSTERS, CPC)
    target_index = jnp.argsort(target_order // PER, stable=True).astype(jnp.int32).reshape(CLUSTERS, CPC)
    source_maps, target_maps = lax.map(one_cluster, (sources[source_index], targets[target_index]))
    source_map = jnp.zeros_like(sources).at[source_index.reshape(-1)].set(source_maps.reshape(-1, D))
    target_map = jnp.zeros_like(targets).at[target_index.reshape(-1)].set(target_maps.reshape(-1, D))
    return source_map, target_map
```

```python
import functools
import math

import jax
import jax.numpy as jnp
from jax import lax
from jax.experimental import pallas as pl
from jax.experimental.pallas import tpu as pltpu
from jax.sharding import PartitionSpec as P

ITERS = 3
entropy_weight = 0.02
LANES = 128
CORES = 2
MESH = pl.DeviceIdType.MESH


def kernel(
    nc, nr, sources, targets, source_order, target_order, source_out, target_out,
    all_s, all_t, sent, maps, back, cost_s, cost_t, potential, source_row, peaks, sums, parts,
    out_send, out_recv, own_send, own_recv, gather_send, gather_recv, part_send, part_recv,
):
    rows, width = sources.shape
    per = rows // nc
    q = nr // nc
    nx = nc // CORES
    columns = all_s.shape[0]
    blocks = columns // LANES
    own_blocks = rows // LANES
    chunks = min(nc, 4)
    group = nc // chunks
    span = rows // chunks
    log_mass = -math.log2(columns)
    scale = math.log2(math.e) / (width * entropy_weight)

    c = lax.axis_index("cluster")
    r = lax.axis_index("row")
    x, core = c // CORES, c % CORES
    k, y = r // q, r % q
    alls = (all_t, all_s)

    def member(mx, mcore, my):
        return (mx * CORES + mcore) * q + my

    def device(mx, mcore, my):
        return (mx * CORES + mcore, k * q + my)

    me = member(x, core, y)

    def line(d):
        return lax.rem(k + d, nc)

    barrier = pltpu.get_barrier_semaphore()
    for d in range(1, nc):
        pl.semaphore_signal(barrier, inc=1, device_id=(c, line(d) * q + y), device_id_type=MESH)
    others = []
    for dx in range(nx):
        for dcore in range(CORES):
            for dy in range(q):
                if dx or dcore or dy:
                    others.append((lax.rem(x + dx, nx), lax.rem(core + dcore, CORES), lax.rem(y + dy, q)))
    for other in others:
        pl.semaphore_signal(barrier, inc=1, device_id=device(*other), device_id_type=MESH)

    def selector(ordering):
        positions = lax.broadcasted_iota(jnp.int32, (rows, rows), 0)
        return (positions == ordering[...]).astype(jnp.float32).astype(jnp.bfloat16)

    def own_rows(t, block, size):
        return alls[t].at[pl.ds(pl.multiple_of(me * rows + block * size, size), size)]

    def into_slots(t, ordering, matrix):
        slots = jnp.dot(selector(ordering), matrix[...], preferred_element_type=jnp.float32)
        sent[t] = slots.astype(jnp.bfloat16)
        own_rows(t, k, per)[...] = sent[t, pl.ds(pl.multiple_of(k * per, per), per)]

    def line_copy(t, d):
        return pltpu.make_async_remote_copy(
            src_ref=sent.at[t, pl.ds(pl.multiple_of(line(d) * per, per), per)],
            dst_ref=own_rows(t, k, per),
            send_sem=own_send.at[t, d],
            recv_sem=own_recv.at[t, d],
            device_id=(c, line(d) * q + y),
            device_id_type=MESH,
        )

    into_slots(0, target_order, targets)
    pl.semaphore_wait(barrier, nc - 1 + nr - 1)
    line_copies = []
    for t in range(2):
        if t == 1:
            into_slots(1, source_order, sources)
        for d in range(1, nc):
            copy = line_copy(t, d)
            copy.start()
            line_copies.append(copy)

    sent_copies = []
    counts = [0, 0]

    def chunk_rows(t, i, owner):
        start = owner * rows + lax.rem(k // group + i, chunks) * span
        return alls[t].at[pl.ds(pl.multiple_of(start, span), span)]

    def forward(t, i, owner, target):
        number = counts[t]
        counts[t] += 1
        owner = member(*owner)
        where = chunk_rows(t, i, owner)
        copy = pltpu.make_async_remote_copy(
            src_ref=where, dst_ref=where,
            send_sem=gather_send.at[t, number], recv_sem=gather_recv.at[t, i, owner],
            device_id=device(*target), device_id_type=MESH,
        )
        copy.start()
        sent_copies.append(copy)

    def arrive(t, i, owner):
        owner = member(*owner)
        where = chunk_rows(t, i, owner)
        pltpu.make_async_remote_copy(
            src_ref=where, dst_ref=where,
            send_sem=gather_send.at[t, 0], recv_sem=gather_recv.at[t, i, owner],
            device_id=device(*others[0]), device_id_type=MESH,
        ).wait_recv()

    def along(i, first, second):
        return (first, second) if i % 2 == 0 else (second, first)

    def at(step, on=None):
        return (lax.rem(x + step[0], nx), core if on is None else on, lax.rem(y + step[1], q))

    def axes(i):
        return (nx, q) if i % 2 == 0 else (q, nx)

    here = (x, core, y)
    sibling_core = CORES - 1 - core
    sibling = (x, sibling_core, y)

    def gather_own(t):
        if group > 1:
            for d in range(1, nc):
                line_copy(t, d).wait_recv()
        for i in range(chunks):
            if group == 1 and i > 0:
                d = nc - i
                pltpu.make_async_remote_copy(
                    src_ref=sent.at[t, pl.ds(0, per)], dst_ref=own_rows(t, line(i), per),
                    send_sem=own_send.at[t, d], recv_sem=own_recv.at[t, d],
                    device_id=(c, line(i) * q + y), device_id_type=MESH,
                ).wait_recv()
            first, second = axes(i)
            for step in range(1, first):
                forward(t, i, here, at(along(i, step, 0)))
            for step in range(1, second):
                forward(t, i, here, at(along(i, 0, step)))
            forward(t, i, here, sibling)

    def gather_first(t):
        for i in range(chunks):
            first, second = axes(i)
            for step in range(1, first):
                owner = at(along(i, step, 0))
                arrive(t, i, owner)
                for turn in range(1, second):
                    forward(t, i, owner, at(along(i, 0, turn)))
                forward(t, i, owner, sibling)

    def gather_second(t):
        for i in range(chunks):
            first, second = axes(i)
            for step in range(first):
                for turn in range(1, second):
                    owner = at(along(i, step, turn))
                    arrive(t, i, owner)
                    forward(t, i, owner, sibling)

    def gather_sibling(t, owner):
        for i in range(chunks):
            arrive(t, i, owner)

    diagonal = lax.broadcasted_iota(jnp.int32, (LANES, LANES), 0) == lax.broadcasted_iota(
        jnp.int32, (LANES, LANES), 1
    )

    def to_row(column):
        spread = jnp.broadcast_to(column, (LANES, LANES))
        return jnp.sum(jnp.where(diagonal, spread, 0.0), axis=0, keepdims=True)

    def to_column(row):
        spread = jnp.broadcast_to(row, (LANES, LANES))
        return jnp.sum(jnp.where(diagonal, spread, 0.0), axis=1, keepdims=True)

    def square_sums(matrix):
        widened = matrix.astype(jnp.float32)
        return jnp.sum(widened * widened, axis=1, keepdims=True)

    def shard(ref, owner):
        return ref[pl.ds(pl.multiple_of(owner * rows, rows), rows)]

    def build(out, own_ref, all_ref, owners):
        own = shard(own_ref, me)
        own_norms = square_sums(own)

        def panel(index, _):
            owner = owners(index)
            other = shard(all_ref, owner)
            inner = lax.dot_general(
                own, other, (((1,), (1,)), ((), ())), preferred_element_type=jnp.float32
            )
            norms = square_sums(other)
            norms = jnp.concatenate(
                [to_row(norms[b * LANES : (b + 1) * LANES]) for b in range(own_blocks)], axis=1
            )
            out[:, pl.ds(pl.multiple_of(owner * rows, rows), rows)] = scale * (
                2.0 * inner - own_norms - norms
            )
            return 0

        return panel

    def row_lse(cost, row):
        norms = []
        for h in range(own_blocks):
            part = pl.ds(h * LANES, LANES)
            peak = None
            for b in range(blocks):
                scores = cost[part, b * LANES : (b + 1) * LANES] + row[b : b + 1, :]
                peak = scores if peak is None else jnp.maximum(peak, scores)
            peak = jnp.max(peak, axis=1, keepdims=True)
            total = jnp.zeros((LANES, LANES), jnp.float32)
            for b in range(blocks):
                scores = cost[part, b * LANES : (b + 1) * LANES] + row[b : b + 1, :]
                total = total + jnp.exp2(scores - peak)
            norms.append(peak + jnp.log2(jnp.sum(total, axis=1, keepdims=True)))
        return norms

    def column_lse(cost, column):
        for b in range(blocks):
            scores = cost[:, b * LANES : (b + 1) * LANES] + column
            peak = jnp.max(scores, axis=0, keepdims=True)
            peaks[b : b + 1, :] = peak
            sums[b : b + 1, :] = jnp.sum(jnp.exp2(scores - peak), axis=0, keepdims=True)
        return peaks[...] + jnp.log2(sums[...])

    def mapped(cost, row, norms, all_ref):
        norms = jnp.concatenate(norms, axis=0)
        total = jnp.zeros((rows, width), jnp.float32)
        step = 4 * LANES
        for start in range(0, columns, step):
            pieces = []
            for b in range(start // LANES, (start + step) // LANES):
                scores = cost[:, b * LANES : (b + 1) * LANES] + row[b : b + 1, :]
                pieces.append(jnp.exp2(scores - norms).astype(jnp.bfloat16))
            total = total + jnp.dot(
                jnp.concatenate(pieces, axis=1),
                all_ref[start : start + step, :],
                preferred_element_type=jnp.float32,
            )
        return total.astype(jnp.bfloat16)

    gather_own(0)
    gather_first(0)
    gather_second(0)
    gather_own(1)
    panel = build(cost_s, all_s, all_t, lambda index: member(
        index // q, core, lax.rem(index, q)))
    lax.fori_loop(0, nx * q, panel, 0)
    for dx in range(nx):
        for dy in range(q):
            gather_sibling(0, at((dx, dy), sibling_core))
    panel = build(cost_s, all_s, all_t, lambda index: member(
        index // q, sibling_core, lax.rem(index, q)))
    lax.fori_loop(0, nx * q, panel, 0)

    potential[...] = jnp.zeros_like(potential)
    part_copies = []
    for repeat in range(ITERS):
        last = repeat == ITERS - 1
        source_potential = [log_mass - norm for norm in row_lse(cost_s, potential)]
        mine = column_lse(cost_s, jnp.concatenate(source_potential, axis=0))
        parts[repeat, me, 0:blocks, :] = mine
        used = blocks
        if last:
            for b in range(own_blocks):
                parts[repeat, me, blocks + b : blocks + b + 1, :] = to_row(source_potential[b])
            used = blocks + own_blocks
        for number, other in enumerate(others):
            copy = pltpu.make_async_remote_copy(
                src_ref=parts.at[repeat, me, pl.ds(0, used)],
                dst_ref=parts.at[repeat, me, pl.ds(0, used)],
                send_sem=part_send.at[repeat, number],
                recv_sem=part_recv.at[repeat, me],
                device_id=device(*other),
                device_id_type=MESH,
            )
            copy.start()
            part_copies.append(copy)
        if repeat == 0:
            gather_first(1)
        if repeat == 1:
            gather_second(1)
        if last:
            for dx in range(nx):
                for dy in range(q):
                    gather_sibling(1, at((dx, dy), sibling_core))
            lax.fori_loop(0, nr, build(cost_t, all_t, all_s, lambda index: index), 0)
        for number, other in enumerate(others):
            owner = member(*other)
            pltpu.make_async_remote_copy(
                src_ref=parts.at[repeat, owner, pl.ds(0, used)],
                dst_ref=parts.at[repeat, owner, pl.ds(0, used)],
                send_sem=part_send.at[repeat, number],
                recv_sem=part_recv.at[repeat, owner],
                device_id=device(*other),
                device_id_type=MESH,
            ).wait_recv()
        each = [parts[repeat, m, 0:blocks, :] for m in range(nr)]
        peak = functools.reduce(jnp.maximum, each)
        column_norm = peak + jnp.log2(sum(jnp.exp2(one - peak) for one in each))
        potential[...] = log_mass - column_norm
        if last:
            sums[...] = column_norm

    def back_copy(t, d):
        return pltpu.make_async_remote_copy(
            src_ref=maps.at[t, pl.ds(pl.multiple_of(line(d) * per, per), per)],
            dst_ref=back.at[t, pl.ds(pl.multiple_of(k * per, per), per)],
            send_sem=out_send.at[t, d],
            recv_sem=out_recv.at[t, d],
            device_id=(c, line(d) * q + y),
            device_id_type=MESH,
        )

    def send_back(t):
        for d in range(1, nc):
            back_copy(t, d).start()
        own = pl.ds(pl.multiple_of(k * per, per), per)
        back[t, own] = maps[t, own]

    maps[1] = mapped(cost_s, potential, row_lse(cost_s, potential), all_t)
    send_back(1)
    for m in range(nr):
        source_row[m * own_blocks : (m + 1) * own_blocks, :] = parts[
            ITERS - 1, m, blocks : blocks + own_blocks, :
        ]
    own_norm = [to_column(sums[pl.ds(me * own_blocks + b, 1), :]) for b in range(own_blocks)]
    maps[0] = mapped(cost_t, source_row, own_norm, all_s)
    send_back(0)

    for copy in line_copies + sent_copies + part_copies:
        copy.wait_send()

    def out_of_slots(t, ordering):
        for d in range(1, nc):
            back_copy(t, d).wait()
        return lax.dot_general(
            selector(ordering), back[t], (((0,), (0,)), ((), ())), preferred_element_type=jnp.float32
        ).astype(jnp.bfloat16)

    source_out[...] = out_of_slots(1, source_order)
    target_out[...] = out_of_slots(0, target_order)


def solution(mesh):
    nc, nr = mesh.shape["cluster"], mesh.shape["row"]

    def shards(sources, targets, source_order, target_order):
        rows, width = sources.shape
        columns = rows * nr
        blocks = columns // LANES
        own_blocks = rows // LANES
        nx, q = nc // CORES, nr // nc
        chunks = min(nc, 4)
        copies = chunks * max(
            a + b - 1 + (a - 1) * b + a * (b - 1) for a, b in ((nx, q), (q, nx))
        )
        vmem = pl.BlockSpec(memory_space=pltpu.VMEM)
        out = jax.ShapeDtypeStruct((rows, width), jnp.bfloat16)
        dma = pltpu.SemaphoreType.DMA
        return pl.pallas_call(
            functools.partial(kernel, nc, nr),
            out_shape=(out, out),
            in_specs=[vmem] * 4,
            out_specs=(vmem, vmem),
            scratch_shapes=[
                pltpu.VMEM((columns, width), jnp.bfloat16),
                pltpu.VMEM((columns, width), jnp.bfloat16),
                pltpu.VMEM((2, rows, width), jnp.bfloat16),
                pltpu.VMEM((2, rows, width), jnp.bfloat16),
                pltpu.VMEM((2, rows, width), jnp.bfloat16),
                pltpu.VMEM((rows, columns), jnp.float32),
                pltpu.VMEM((rows, columns), jnp.float32),
                pltpu.VMEM((blocks, LANES), jnp.float32),
                pltpu.VMEM((blocks, LANES), jnp.float32),
                pltpu.VMEM((blocks, LANES), jnp.float32),
                pltpu.VMEM((blocks, LANES), jnp.float32),
                pltpu.VMEM((ITERS, nr, blocks + 8, LANES), jnp.float32),
                dma((2, nc)), dma((2, nc)), dma((2, nc)), dma((2, nc)),
                dma((2, copies)), dma((2, chunks, nr)),
                dma((ITERS, nr)), dma((ITERS, nr)),
            ],
            compiler_params=pltpu.CompilerParams(
                collective_id=0, has_side_effects=True, vmem_limit_bytes=48 * 1024 * 1024
            ),
        )(sources, targets, source_order.reshape(1, rows), target_order.reshape(1, rows))

    return jax.shard_map(
        shards,
        mesh=mesh,
        in_specs=(
            P(("cluster", "row"), None),
            P(("cluster", "row"), None),
            P(("cluster", "row")),
            P(("cluster", "row")),
        ),
        out_specs=(P(("cluster", "row"), None), P(("cluster", "row"), None)),
        check_vma=False,
    )
```

```python
import functools
import math

import jax
import jax.numpy as jnp
from jax import lax
from jax.experimental import pallas as pl
from jax.experimental.pallas import tpu as pltpu
from jax.sharding import PartitionSpec as P

ITERS = 3
entropy_weight = 0.02
LANES = 128
CORES = 2
MESH = pl.DeviceIdType.MESH


def kernel(
    nc, nr, sources, targets, source_order, target_order, source_out, target_out,
    given, all_s, all_t, sent, maps, back, cost_s, cost_t, target_norms, potential, source_row,
    peaks, sums, parts, in_sem, out_send, out_recv, own_send, own_recv, gather_send, gather_recv, part_send, part_recv,
):
    rows, width = sources.shape
    per = rows // nc
    q = nr // nc
    nx = nc // CORES
    columns = all_s.shape[0]
    blocks = columns // LANES
    own_blocks = rows // LANES
    chunks = min(nc, 4)
    group = nc // chunks
    span = rows // chunks
    log_mass = -math.log2(columns)
    scale = math.log2(math.e) / (width * entropy_weight)

    c = lax.axis_index("cluster")
    r = lax.axis_index("row")
    x, core = c // CORES, c % CORES
    k, y = r // q, r % q
    alls = (all_t, all_s)

    def member(mx, mcore, my):
        return (mx * CORES + mcore) * q + my

    def device(mx, mcore, my):
        return (mx * CORES + mcore, k * q + my)

    me = member(x, core, y)

    def line(d):
        return lax.rem(k + d, nc)

    reads = [
        pltpu.make_async_copy(ref, given.at[t], in_sem.at[t]) for t, ref in enumerate((targets, sources))
    ]
    for read in reads:
        read.start()

    barrier = pltpu.get_barrier_semaphore()
    for d in range(1, nc):
        pl.semaphore_signal(barrier, inc=1, device_id=(c, line(d) * q + y), device_id_type=MESH)
    others = []
    for dx in range(nx):
        for dcore in range(CORES):
            for dy in range(q):
                if dx or dcore or dy:
                    others.append((lax.rem(x + dx, nx), lax.rem(core + dcore, CORES), lax.rem(y + dy, q)))
    for other in others:
        pl.semaphore_signal(barrier, inc=1, device_id=device(*other), device_id_type=MESH)

    def selector(ordering):
        positions = lax.broadcasted_iota(jnp.int32, (rows, rows), 0)
        return (positions == ordering[...]).astype(jnp.float32).astype(jnp.bfloat16)

    def own_rows(t, block, owner=me):
        return alls[t].at[pl.ds(pl.multiple_of(owner * rows + block * per, per), per)]

    def into_slots(t, ordering):
        reads[t].wait()
        slots = jnp.dot(selector(ordering), given[t], preferred_element_type=jnp.float32)
        sent[t] = slots.astype(jnp.bfloat16)
        own_rows(t, 0)[...] = sent[t, pl.ds(pl.multiple_of(k * per, per), per)]

    def line_copy(t, d):
        return pltpu.make_async_remote_copy(
            src_ref=sent.at[t, pl.ds(pl.multiple_of(line(d) * per, per), per)],
            dst_ref=own_rows(t, nc - d),
            send_sem=own_send.at[t, d],
            recv_sem=own_recv.at[t, d],
            device_id=(c, line(d) * q + y),
            device_id_type=MESH,
        )

    into_slots(0, target_order)
    pl.semaphore_wait(barrier, nc - 1 + nr - 1)
    line_copies = []
    for t in range(2):
        if t == 1:
            into_slots(1, source_order)
        for d in range(1, nc):
            copy = line_copy(t, d)
            copy.start()
            line_copies.append(copy)

    sent_copies = []
    counts = [0, 0]

    def chunk_rows(t, i, owner):
        start = owner * rows + i * span
        return alls[t].at[pl.ds(pl.multiple_of(start, span), span)]

    def forward(t, i, owner, target):
        number = counts[t]
        counts[t] += 1
        owner = member(*owner)
        where = chunk_rows(t, i, owner)
        copy = pltpu.make_async_remote_copy(
            src_ref=where, dst_ref=where,
            send_sem=gather_send.at[t, number], recv_sem=gather_recv.at[t, i, owner],
            device_id=device(*target), device_id_type=MESH,
        )
        copy.start()
        sent_copies.append(copy)

    def arrive(t, i, owner):
        owner = member(*owner)
        where = chunk_rows(t, i, owner)
        pltpu.make_async_remote_copy(
            src_ref=where, dst_ref=where,
            send_sem=gather_send.at[t, 0], recv_sem=gather_recv.at[t, i, owner],
            device_id=device(*others[0]), device_id_type=MESH,
        ).wait_recv()

    def along(i, first, second):
        return (first, second) if i % 2 == 0 else (second, first)

    def at(step, on=None):
        return (lax.rem(x + step[0], nx), core if on is None else on, lax.rem(y + step[1], q))

    def axes(i):
        return (nx, q) if i % 2 == 0 else (q, nx)

    here = (x, core, y)
    sibling_core = CORES - 1 - core
    sibling = (x, sibling_core, y)

    def gather_own(t, after=None):
        for i in range(chunks):
            for j in range(i * group, (i + 1) * group):
                if j > 0:
                    pltpu.make_async_remote_copy(
                        src_ref=sent.at[t, pl.ds(0, per)], dst_ref=own_rows(t, j),
                        send_sem=own_send.at[t, nc - j], recv_sem=own_recv.at[t, nc - j],
                        device_id=(c, line(j) * q + y), device_id_type=MESH,
                    ).wait_recv()
            first, second = axes(i)
            for step in range(1, first):
                forward(t, i, here, at(along(i, step, 0)))
            for step in range(1, second):
                forward(t, i, here, at(along(i, 0, step)))
            forward(t, i, here, sibling)
            if after is not None:
                after((i + 1) * span)

    def gather_first(t):
        for i in range(chunks):
            first, second = axes(i)
            for step in range(1, first):
                owner = at(along(i, step, 0))
                arrive(t, i, owner)
                for turn in range(1, second):
                    forward(t, i, owner, at(along(i, 0, turn)))
                forward(t, i, owner, sibling)

    def gather_second(t):
        for i in range(chunks):
            first, second = axes(i)
            for step in range(first):
                for turn in range(1, second):
                    owner = at(along(i, step, turn))
                    arrive(t, i, owner)
                    forward(t, i, owner, sibling)

    def gather_sibling(t, owner):
        for i in range(chunks):
            arrive(t, i, owner)

    diagonal = lax.broadcasted_iota(jnp.int32, (LANES, LANES), 0) == lax.broadcasted_iota(
        jnp.int32, (LANES, LANES), 1
    )

    def to_row(column):
        spread = jnp.broadcast_to(column, (LANES, LANES))
        return jnp.sum(jnp.where(diagonal, spread, 0.0), axis=0, keepdims=True)

    def to_column(row):
        spread = jnp.broadcast_to(row, (LANES, LANES))
        return jnp.sum(jnp.where(diagonal, spread, 0.0), axis=1, keepdims=True)

    def square_sums(matrix):
        widened = matrix.astype(jnp.float32)
        return jnp.sum(widened * widened, axis=1, keepdims=True)

    def shard(ref, owner):
        return ref[pl.ds(pl.multiple_of(owner * rows, rows), rows)]

    def norms_row(matrix):
        norms = square_sums(matrix)
        return [to_row(norms[b * LANES : (b + 1) * LANES]) for b in range(own_blocks)]

    def build_sources(part):
        own = all_s[pl.ds(pl.multiple_of(me * rows + part * LANES, LANES), LANES)]
        own_norms = square_sums(own)
        for m in range(nr):
            inner = lax.dot_general(
                own, all_t[m * rows : (m + 1) * rows, :], (((1,), (1,)), ((), ())),
                preferred_element_type=jnp.float32,
            )
            for b in range(own_blocks):
                block = m * own_blocks + b
                cost_s[part * LANES : (part + 1) * LANES, block * LANES : (block + 1) * LANES] = scale * (
                    2.0 * inner[:, b * LANES : (b + 1) * LANES]
                    - own_norms - target_norms[block : block + 1, :]
                )

    def build_targets(which):
        own = shard(all_t, me)
        own_norms = square_sums(own)

        def panel(index, _):
            owner = member(index // q, which, lax.rem(index, q))
            other = shard(all_s, owner)
            inner = lax.dot_general(
                own, other, (((1,), (1,)), ((), ())), preferred_element_type=jnp.float32
            )
            norms = jnp.concatenate(norms_row(other), axis=1)
            cost_t[:, pl.ds(pl.multiple_of(owner * rows, rows), rows)] = scale * (
                2.0 * inner - own_norms - norms
            )
            return 0

        lax.fori_loop(0, nx * q, panel, 0)

    def norm_targets(which):
        def panel(index, _):
            owner = member(index // q, which, lax.rem(index, q))
            for b, norms in enumerate(norms_row(shard(all_t, owner))):
                target_norms[pl.ds(owner * own_blocks + b, 1), :] = norms
            return 0

        lax.fori_loop(0, nx * q, panel, 0)

    def row_lse(cost, row, h):
        part = pl.ds(h * LANES, LANES)
        peak = None
        for b in range(blocks):
            scores = cost[part, b * LANES : (b + 1) * LANES] + row[b : b + 1, :]
            peak = scores if peak is None else jnp.maximum(peak, scores)
        peak = jnp.max(peak, axis=1, keepdims=True)
        total = jnp.zeros((LANES, LANES), jnp.float32)
        for b in range(blocks):
            scores = cost[part, b * LANES : (b + 1) * LANES] + row[b : b + 1, :]
            total = total + jnp.exp2(scores - peak)
        return peak + jnp.log2(jnp.sum(total, axis=1, keepdims=True))

    def column_lse(cost, column):
        for b in range(blocks):
            scores = cost[:, b * LANES : (b + 1) * LANES] + column
            peak = jnp.max(scores, axis=0, keepdims=True)
            peaks[b : b + 1, :] = peak
            sums[b : b + 1, :] = jnp.sum(jnp.exp2(scores - peak), axis=0, keepdims=True)
        return peaks[...] + jnp.log2(sums[...])

    def mapped(cost, row, norm, all_ref, h):
        part = pl.ds(h * LANES, LANES)
        total = jnp.zeros((LANES, width), jnp.float32)
        step = 4 * LANES
        for start in range(0, columns, step):
            pieces = []
            for b in range(start // LANES, (start + step) // LANES):
                scores = cost[part, b * LANES : (b + 1) * LANES] + row[b : b + 1, :]
                pieces.append(jnp.exp2(scores - norm).astype(jnp.bfloat16))
            total = total + jnp.dot(
                jnp.concatenate(pieces, axis=1),
                all_ref[start : start + step, :],
                preferred_element_type=jnp.float32,
            )
        return total.astype(jnp.bfloat16)

    gather_own(0)
    gather_first(0)
    gather_second(0)
    norm_targets(core)
    for dx in range(nx):
        for dy in range(q):
            gather_sibling(0, at((dx, dy), sibling_core))
    norm_targets(sibling_core)

    potential[...] = jnp.zeros_like(potential)
    first_norms = []

    def first_rows(arrived):
        while len(first_norms) < arrived // LANES:
            build_sources(len(first_norms))
            first_norms.append(row_lse(cost_s, potential, len(first_norms)))

    gather_own(1, first_rows)
    part_copies = []
    for repeat in range(ITERS):
        last = repeat == ITERS - 1
        if repeat == 0:
            norms = first_norms
        else:
            norms = [row_lse(cost_s, potential, h) for h in range(own_blocks)]
        source_potential = [log_mass - norm for norm in norms]
        mine = column_lse(cost_s, jnp.concatenate(source_potential, axis=0))
        parts[repeat, me, 0:blocks, :] = mine
        used = blocks
        if last:
            for b in range(own_blocks):
                parts[repeat, me, blocks + b : blocks + b + 1, :] = to_row(source_potential[b])
            used = blocks + own_blocks
        for number, other in enumerate(others):
            copy = pltpu.make_async_remote_copy(
                src_ref=parts.at[repeat, me, pl.ds(0, used)],
                dst_ref=parts.at[repeat, me, pl.ds(0, used)],
                send_sem=part_send.at[repeat, number],
                recv_sem=part_recv.at[repeat, me],
                device_id=device(*other),
                device_id_type=MESH,
            )
            copy.start()
            part_copies.append(copy)
        if repeat == 0:
            gather_first(1)
        if repeat == 1:
            gather_second(1)
            build_targets(core)
        if last:
            for dx in range(nx):
                for dy in range(q):
                    gather_sibling(1, at((dx, dy), sibling_core))
            build_targets(sibling_core)
        for number, other in enumerate(others):
            owner = member(*other)
            pltpu.make_async_remote_copy(
                src_ref=parts.at[repeat, owner, pl.ds(0, used)],
                dst_ref=parts.at[repeat, owner, pl.ds(0, used)],
                send_sem=part_send.at[repeat, number],
                recv_sem=part_recv.at[repeat, owner],
                device_id=device(*other),
                device_id_type=MESH,
            ).wait_recv()
        each = [parts[repeat, m, 0:blocks, :] for m in range(nr)]
        peak = functools.reduce(jnp.maximum, each)
        column_norm = peak + jnp.log2(sum(jnp.exp2(one - peak) for one in each))
        potential[...] = log_mass - column_norm
        if last:
            sums[...] = column_norm

    def back_copy(t, d):
        return pltpu.make_async_remote_copy(
            src_ref=maps.at[t, d * per : (d + 1) * per],
            dst_ref=back.at[t, pl.ds(pl.multiple_of(k * per, per), per)],
            send_sem=out_send.at[t, d],
            recv_sem=out_recv.at[t, d],
            device_id=(c, line(d) * q + y),
            device_id_type=MESH,
        )

    def send_back(t, h, result):
        maps[t, h * LANES : (h + 1) * LANES] = result
        for d in range(h * LANES // per, (h + 1) * LANES // per):
            if d > 0:
                back_copy(t, d).start()
            else:
                back[t, pl.ds(pl.multiple_of(k * per, per), per)] = maps[t, 0:per]

    for m in range(nr):
        source_row[m * own_blocks : (m + 1) * own_blocks, :] = parts[
            ITERS - 1, m, blocks : blocks + own_blocks, :
        ]
    for h in reversed(range(own_blocks)):
        norm = to_column(sums[pl.ds(me * own_blocks + h, 1), :])
        send_back(0, h, mapped(cost_t, source_row, norm, all_s, h))
    for h in reversed(range(own_blocks)):
        norm = row_lse(cost_s, potential, h)
        send_back(1, h, mapped(cost_s, potential, norm, all_t, h))

    for copy in line_copies + sent_copies + part_copies:
        copy.wait_send()

    def out_of_slots(t, ordering):
        for d in range(1, nc):
            back_copy(t, d).wait()
        return lax.dot_general(
            selector(ordering), back[t], (((0,), (0,)), ((), ())), preferred_element_type=jnp.float32
        ).astype(jnp.bfloat16)

    writes = []
    for t, (ordering, out) in enumerate(((target_order, target_out), (source_order, source_out))):
        given[t] = out_of_slots(t, ordering)
        write = pltpu.make_async_copy(given.at[t], out, in_sem.at[t])
        write.start()
        writes.append(write)
    for write in writes:
        write.wait()


def solution(mesh):
    nc, nr = mesh.shape["cluster"], mesh.shape["row"]

    def shards(sources, targets, source_order, target_order):
        rows, width = sources.shape
        columns = rows * nr
        blocks = columns // LANES
        own_blocks = rows // LANES
        nx, q = nc // CORES, nr // nc
        chunks = min(nc, 4)
        copies = chunks * max(
            a + b - 1 + (a - 1) * b + a * (b - 1) for a, b in ((nx, q), (q, nx))
        )
        vmem = pl.BlockSpec(memory_space=pltpu.VMEM)
        out = jax.ShapeDtypeStruct((rows, width), jnp.bfloat16)
        dma = pltpu.SemaphoreType.DMA
        return pl.pallas_call(
            functools.partial(kernel, nc, nr),
            out_shape=(out, out),
            in_specs=[pl.BlockSpec(memory_space=pl.ANY)] * 2 + [vmem] * 2,
            out_specs=(pl.BlockSpec(memory_space=pl.ANY),) * 2,
            scratch_shapes=[
                pltpu.VMEM((2, rows, width), jnp.bfloat16),
                pltpu.VMEM((columns, width), jnp.bfloat16),
                pltpu.VMEM((columns, width), jnp.bfloat16),
                pltpu.VMEM((2, rows, width), jnp.bfloat16),
                pltpu.VMEM((2, rows, width), jnp.bfloat16),
                pltpu.VMEM((2, rows, width), jnp.bfloat16),
                pltpu.VMEM((rows, columns), jnp.float32),
                pltpu.VMEM((rows, columns), jnp.float32),
                pltpu.VMEM((blocks, LANES), jnp.float32),
                pltpu.VMEM((blocks, LANES), jnp.float32),
                pltpu.VMEM((blocks, LANES), jnp.float32),
                pltpu.VMEM((blocks, LANES), jnp.float32),
                pltpu.VMEM((blocks, LANES), jnp.float32),
                pltpu.VMEM((ITERS, nr, blocks + 8, LANES), jnp.float32),
                dma((2,)), dma((2, nc)), dma((2, nc)), dma((2, nc)), dma((2, nc)),
                dma((2, copies)), dma((2, chunks, nr)),
                dma((ITERS, nr)), dma((ITERS, nr)),
            ],
            compiler_params=pltpu.CompilerParams(
                collective_id=0, has_side_effects=True, vmem_limit_bytes=63 * 1024 * 1024
            ),
        )(sources, targets, source_order.reshape(1, rows), target_order.reshape(1, rows))

    return jax.shard_map(
        shards,
        mesh=mesh,
        in_specs=(
            P(("cluster", "row"), None),
            P(("cluster", "row"), None),
            P(("cluster", "row")),
            P(("cluster", "row")),
        ),
        out_specs=(P(("cluster", "row"), None), P(("cluster", "row"), None)),
        check_vma=False,
    )
```

```python
import functools
import math

import jax
import jax.numpy as jnp
from jax import lax
from jax.experimental import pallas as pl
from jax.experimental.pallas import tpu as pltpu
from jax.sharding import PartitionSpec as P

ITERS = 3
entropy_weight = 0.02
LANES = 128
CORES = 2
MESH = pl.DeviceIdType.MESH


def kernel(
    nc, nr, sources, targets, source_order, target_order, source_out, target_out,
    given, alls, sent, maps, back, cost, square_rows, potentials, norms, peaks, sums, parts,
    in_sem, out_send, out_recv, own_send, own_recv, gather_send, gather_recv, part_send, part_recv,
):
    rows, width = sources.shape
    per = rows // nc
    q = nr // nc
    nx = nc // CORES
    columns = alls.shape[1]
    blocks = columns // LANES
    own_blocks = rows // LANES
    chunks = min(nc, 4)
    group = nc // chunks
    span = rows // chunks
    log_mass = -math.log2(columns)
    scale = math.log2(math.e) / (width * entropy_weight)

    c = lax.axis_index("cluster")
    r = lax.axis_index("row")
    x, core = c // CORES, c % CORES
    k, y = r // q, r % q

    def member(mx, mcore, my):
        return (mx * CORES + mcore) * q + my

    def device(mx, mcore, my):
        return (mx * CORES + mcore, k * q + my)

    me = member(x, core, y)

    def line(d):
        return lax.rem(k + d, nc)

    reads = [
        pltpu.make_async_copy(ref, given.at[t], in_sem.at[t]) for t, ref in enumerate((targets, sources))
    ]
    for read in reads:
        read.start()

    barrier = pltpu.get_barrier_semaphore()
    for d in range(1, nc):
        pl.semaphore_signal(barrier, inc=1, device_id=(c, line(d) * q + y), device_id_type=MESH)
    others = []
    for dx in range(nx):
        for dcore in range(CORES):
            for dy in range(q):
                if dx or dcore or dy:
                    others.append((lax.rem(x + dx, nx), lax.rem(core + dcore, CORES), lax.rem(y + dy, q)))
    for other in others:
        pl.semaphore_signal(barrier, inc=1, device_id=device(*other), device_id_type=MESH)

    def selector(ordering):
        positions = lax.broadcasted_iota(jnp.int32, (rows, rows), 0)
        return (positions == ordering[...]).astype(jnp.float32).astype(jnp.bfloat16)

    def own_rows(t, block, owner=me):
        return alls.at[t, pl.ds(pl.multiple_of(owner * rows + block * per, per), per)]

    def into_slots(t, ordering):
        reads[t].wait()
        slots = jnp.dot(selector(ordering), given[t], preferred_element_type=jnp.float32)
        sent[t] = slots.astype(jnp.bfloat16)
        own_rows(t, 0)[...] = sent[t, pl.ds(pl.multiple_of(k * per, per), per)]

    def line_copy(t, d):
        return pltpu.make_async_remote_copy(
            src_ref=sent.at[t, pl.ds(pl.multiple_of(line(d) * per, per), per)],
            dst_ref=own_rows(t, nc - d),
            send_sem=own_send.at[t, d],
            recv_sem=own_recv.at[t, d],
            device_id=(c, line(d) * q + y),
            device_id_type=MESH,
        )

    into_slots(0, target_order)
    pl.semaphore_wait(barrier, nc - 1 + nr - 1)
    line_copies = []
    for t in range(2):
        if t == 1:
            into_slots(1, source_order)
        for d in range(1, nc):
            copy = line_copy(t, d)
            copy.start()
            line_copies.append(copy)

    counts = [0, 0]

    def chunk_rows(t, i, owner):
        start = owner * rows + i * span
        return alls.at[t, pl.ds(pl.multiple_of(start, span), span)]

    def forward(t, i, owner, target):
        number = counts[t]
        counts[t] += 1
        owner = member(*owner)
        where = chunk_rows(t, i, owner)
        copy = pltpu.make_async_remote_copy(
            src_ref=where, dst_ref=where,
            send_sem=gather_send.at[t, number], recv_sem=gather_recv.at[t, i, owner],
            device_id=device(*target), device_id_type=MESH,
        )
        copy.start()

    def arrive(t, i, owner):
        owner = member(*owner)
        where = chunk_rows(t, i, owner)
        pltpu.make_async_remote_copy(
            src_ref=where, dst_ref=where,
            send_sem=gather_send.at[t, 0], recv_sem=gather_recv.at[t, i, owner],
            device_id=device(*others[0]), device_id_type=MESH,
        ).wait_recv()

    def along(i, first, second):
        return (first, second) if i % 2 == 0 else (second, first)

    def at(step, on=None):
        return (lax.rem(x + step[0], nx), core if on is None else on, lax.rem(y + step[1], q))

    def axes(i):
        return (nx, q) if i % 2 == 0 else (q, nx)

    here = (x, core, y)
    sibling_core = CORES - 1 - core
    sibling = (x, sibling_core, y)

    def gather_own(t):
        for i in range(chunks):
            for j in range(i * group, (i + 1) * group):
                if j > 0:
                    pltpu.make_async_remote_copy(
                        src_ref=sent.at[t, pl.ds(0, per)], dst_ref=own_rows(t, j),
                        send_sem=own_send.at[t, nc - j], recv_sem=own_recv.at[t, nc - j],
                        device_id=(c, line(j) * q + y), device_id_type=MESH,
                    ).wait_recv()
            first, second = axes(i)
            for step in range(1, first):
                forward(t, i, here, at(along(i, step, 0)))
            for step in range(1, second):
                forward(t, i, here, at(along(i, 0, step)))
            forward(t, i, here, sibling)

    def gather_first(t):
        for i in range(chunks):
            first, second = axes(i)
            for step in range(1, first):
                owner = at(along(i, step, 0))
                arrive(t, i, owner)
                for turn in range(1, second):
                    forward(t, i, owner, at(along(i, 0, turn)))
                forward(t, i, owner, sibling)

    def gather_second(t):
        for i in range(chunks):
            first, second = axes(i)
            for step in range(first):
                for turn in range(1, second):
                    owner = at(along(i, step, turn))
                    arrive(t, i, owner)
                    forward(t, i, owner, sibling)

    def gather_sibling(t, owner):
        for i in range(chunks):
            arrive(t, i, owner)

    diagonal = lax.broadcasted_iota(jnp.int32, (LANES, LANES), 0) == lax.broadcasted_iota(
        jnp.int32, (LANES, LANES), 1
    )

    def to_row(column):
        spread = jnp.broadcast_to(column, (LANES, LANES))
        return jnp.sum(jnp.where(diagonal, spread, 0.0), axis=0, keepdims=True)

    def to_column(row):
        spread = jnp.broadcast_to(row, (LANES, LANES))
        return jnp.sum(jnp.where(diagonal, spread, 0.0), axis=1, keepdims=True)

    def square_sums(matrix):
        widened = matrix.astype(jnp.float32)
        return jnp.sum(widened * widened, axis=1, keepdims=True)

    def shard(t, owner):
        return alls[t, pl.ds(pl.multiple_of(owner * rows, rows), rows)]

    def over_members(which, body):
        def step(index, _):
            body(member(index // q, which, lax.rem(index, q)))
            return 0

        lax.fori_loop(0, nx * q, step, 0)

    def square_panels(t, which):
        def panel(owner):
            squares = square_sums(shard(t, owner))
            for b in range(own_blocks):
                square_rows[t, pl.ds(owner * own_blocks + b, 1), :] = to_row(
                    squares[b * LANES : (b + 1) * LANES]
                )

        over_members(which, panel)

    def build(t, which):
        own = shard(t, me)
        own_squares = square_sums(own)

        def panel(owner):
            inner = lax.dot_general(
                own, shard(1 - t, owner), (((1,), (1,)), ((), ())),
                preferred_element_type=jnp.float32,
            )
            squares = jnp.concatenate(
                [square_rows[1 - t, pl.ds(owner * own_blocks + b, 1), :] for b in range(own_blocks)],
                axis=1,
            )
            cost[t, :, pl.ds(pl.multiple_of(owner * rows, rows), rows)] = scale * (
                2.0 * inner - own_squares - squares
            )

        over_members(which, panel)

    def row_pass():
        def half(h, _):
            part = pl.ds(pl.multiple_of(h * LANES, LANES), LANES)

            def scores(b):
                return cost[1, part, b * LANES : (b + 1) * LANES] + potentials[1, b : b + 1, :]

            peak = functools.reduce(jnp.maximum, (scores(b) for b in range(blocks)))
            peak = jnp.max(peak, axis=1, keepdims=True)
            total = jnp.zeros((LANES, LANES), jnp.float32)
            for b in range(blocks):
                total = total + jnp.exp2(scores(b) - peak)
            norm = peak + jnp.log2(jnp.sum(total, axis=1, keepdims=True))
            norms[1, part, :] = jnp.broadcast_to(norm, (LANES, LANES))
            return 0

        lax.fori_loop(0, own_blocks, half, 0)

    def column_pass():
        def block(b, _):
            lanes = pl.ds(pl.multiple_of(b * LANES, LANES), LANES)
            scores = cost[1, :, lanes] + (log_mass - norms[1])
            peak = jnp.max(scores, axis=0, keepdims=True)
            peaks[pl.ds(b, 1), :] = peak
            sums[pl.ds(b, 1), :] = jnp.sum(jnp.exp2(scores - peak), axis=0, keepdims=True)
            return 0

        lax.fori_loop(0, blocks, block, 0, unroll=2)
        return peaks[...] + jnp.log2(sums[...])

    def part_copy(repeat, number, owner):
        where = parts.at[repeat, owner, pl.ds(0, blocks + own_blocks)]
        return pltpu.make_async_remote_copy(
            src_ref=where,
            dst_ref=where,
            send_sem=part_send.at[repeat, number],
            recv_sem=part_recv.at[repeat, owner],
            device_id=device(*others[number]),
            device_id_type=MESH,
        )

    gather_own(0)
    gather_first(0)
    gather_second(0)
    square_panels(0, core)
    for dx in range(nx):
        for dy in range(q):
            gather_sibling(0, at((dx, dy), sibling_core))
    square_panels(0, sibling_core)
    gather_own(1)
    build(1, core)
    build(1, sibling_core)

    potentials[1] = jnp.zeros_like(potentials[1])

    def iteration(repeat, _):
        row_pass()
        parts[repeat, me, 0:blocks, :] = column_pass()
        for b in range(own_blocks):
            parts[repeat, me, blocks + b : blocks + b + 1, :] = to_row(
                log_mass - norms[1, b * LANES : (b + 1) * LANES, :]
            )
        for number in range(len(others)):
            part_copy(repeat, number, me).start()

        @pl.when(repeat == 0)
        def _():
            gather_first(1)

        @pl.when(repeat == 1)
        def _():
            gather_second(1)
            square_panels(1, core)
            build(0, core)

        @pl.when(repeat == ITERS - 1)
        def _():
            for dx in range(nx):
                for dy in range(q):
                    gather_sibling(1, at((dx, dy), sibling_core))
            square_panels(1, sibling_core)
            build(0, sibling_core)

        for number, other in enumerate(others):
            part_copy(repeat, number, member(*other)).wait_recv()
        each = [parts[repeat, m, 0:blocks, :] for m in range(nr)]
        peak = functools.reduce(jnp.maximum, each)
        column_norm = peak + jnp.log2(sum(jnp.exp2(one - peak) for one in each))
        potentials[1] = log_mass - column_norm
        sums[...] = column_norm
        return 0

    lax.fori_loop(0, ITERS, iteration, 0)

    def back_copy(t, d):
        return pltpu.make_async_remote_copy(
            src_ref=maps.at[t, pl.ds(pl.multiple_of(d * per, per), per)],
            dst_ref=back.at[t, pl.ds(pl.multiple_of(k * per, per), per)],
            send_sem=out_send.at[t, d],
            recv_sem=out_recv.at[t, d],
            device_id=(c, line(d) * q + y),
            device_id_type=MESH,
        )

    for m in range(nr):
        potentials[0, m * own_blocks : (m + 1) * own_blocks, :] = parts[
            ITERS - 1, m, blocks : blocks + own_blocks, :
        ]
    for b in range(own_blocks):
        norms[0, b * LANES : (b + 1) * LANES, :] = jnp.broadcast_to(
            to_column(sums[pl.ds(me * own_blocks + b, 1), :]), (LANES, LANES)
        )

    def mapped(t, h):
        part = pl.ds(pl.multiple_of(h * LANES, LANES), LANES)
        total = jnp.zeros((LANES, width), jnp.float32)
        step = 4 * LANES
        for start in range(0, columns, step):
            pieces = []
            for b in range(start // LANES, (start + step) // LANES):
                scores = cost[t, part, b * LANES : (b + 1) * LANES] + potentials[t, b : b + 1, :]
                pieces.append(jnp.exp2(scores - norms[t, part, :]).astype(jnp.bfloat16))
            total = total + jnp.dot(
                jnp.concatenate(pieces, axis=1),
                alls[1 - t, start : start + step, :],
                preferred_element_type=jnp.float32,
            )
        maps[t, part] = total.astype(jnp.bfloat16)
        for j in range(LANES // per):
            d = h * (LANES // per) + j

            @pl.when(d > 0)
            def _():
                back_copy(t, d).start()

    def both_maps(t, _):
        @pl.when(t == 1)
        def _():
            row_pass()

        def half(j, _):
            mapped(t, own_blocks - 1 - j)
            return 0

        lax.fori_loop(0, own_blocks, half, 0)
        back[t, pl.ds(pl.multiple_of(k * per, per), per)] = maps[t, 0:per]
        return 0

    lax.fori_loop(0, 2, both_maps, 0)

    for copy in line_copies:
        copy.wait_send()
    for t in range(2):
        for number in range(counts[t]):
            pltpu.make_async_remote_copy(
                src_ref=chunk_rows(t, 0, me), dst_ref=chunk_rows(t, 0, me),
                send_sem=gather_send.at[t, number], recv_sem=gather_recv.at[t, 0, me],
                device_id=device(*others[0]), device_id_type=MESH,
            ).wait_send()
    for repeat in range(ITERS):
        for number in range(len(others)):
            part_copy(repeat, number, me).wait_send()

    def out_of_slots(t, ordering):
        for d in range(1, nc):
            back_copy(t, d).wait()
        return lax.dot_general(
            selector(ordering), back[t], (((0,), (0,)), ((), ())), preferred_element_type=jnp.float32
        ).astype(jnp.bfloat16)

    writes = []
    for t, (ordering, out) in enumerate(((target_order, target_out), (source_order, source_out))):
        given[t] = out_of_slots(t, ordering)
        write = pltpu.make_async_copy(given.at[t], out, in_sem.at[t])
        write.start()
        writes.append(write)
    for write in writes:
        write.wait()


def solution(mesh):
    nc, nr = mesh.shape["cluster"], mesh.shape["row"]

    def shards(sources, targets, source_order, target_order):
        rows, width = sources.shape
        columns = rows * nr
        blocks = columns // LANES
        own_blocks = rows // LANES
        nx, q = nc // CORES, nr // nc
        chunks = min(nc, 4)
        copies = chunks * max(
            a + b - 1 + (a - 1) * b + a * (b - 1) for a, b in ((nx, q), (q, nx))
        )
        vmem = pl.BlockSpec(memory_space=pltpu.VMEM)
        out = jax.ShapeDtypeStruct((rows, width), jnp.bfloat16)
        dma = pltpu.SemaphoreType.DMA
        return pl.pallas_call(
            functools.partial(kernel, nc, nr),
            out_shape=(out, out),
            in_specs=[pl.BlockSpec(memory_space=pl.ANY)] * 2 + [vmem] * 2,
            out_specs=(pl.BlockSpec(memory_space=pl.ANY),) * 2,
            scratch_shapes=[
                pltpu.VMEM((2, rows, width), jnp.bfloat16),
                pltpu.VMEM((2, columns, width), jnp.bfloat16),
                pltpu.VMEM((2, rows, width), jnp.bfloat16),
                pltpu.VMEM((2, rows, width), jnp.bfloat16),
                pltpu.VMEM((2, rows, width), jnp.bfloat16),
                pltpu.VMEM((2, rows, columns), jnp.float32),
                pltpu.VMEM((2, blocks, LANES), jnp.float32),
                pltpu.VMEM((2, blocks, LANES), jnp.float32),
                pltpu.VMEM((2, rows, LANES), jnp.float32),
                pltpu.VMEM((blocks, LANES), jnp.float32),
                pltpu.VMEM((blocks, LANES), jnp.float32),
                pltpu.VMEM((ITERS, nr, blocks + 8, LANES), jnp.float32),
                dma((2,)), dma((2, nc)), dma((2, nc)), dma((2, nc)), dma((2, nc)),
                dma((2, copies)), dma((2, chunks, nr)),
                dma((ITERS, nr)), dma((ITERS, nr)),
            ],
            compiler_params=pltpu.CompilerParams(
                collective_id=0, has_side_effects=True, vmem_limit_bytes=63 * 1024 * 1024
            ),
        )(sources, targets, source_order.reshape(1, rows), target_order.reshape(1, rows))

    return jax.shard_map(
        shards,
        mesh=mesh,
        in_specs=(
            P(("cluster", "row"), None),
            P(("cluster", "row"), None),
            P(("cluster", "row")),
            P(("cluster", "row")),
        ),
        out_specs=(P(("cluster", "row"), None), P(("cluster", "row"), None)),
        check_vma=False,
    )
```

```python
import functools
import math

import jax
import jax.numpy as jnp
from jax import lax
from jax.experimental import pallas as pl
from jax.experimental.pallas import tpu as pltpu
from jax.sharding import PartitionSpec as P

ITERS = 3
entropy_weight = 0.02
LANES = 128
CORES = 2
MESH = pl.DeviceIdType.MESH


def kernel(
    nc, nr, sources, targets, source_order, target_order, source_out, target_out,
    alls, sent, maps, back, cost, square_rows, potentials, norms, peaks, sums, parts,
    out_send, out_recv, own_send, own_recv, gather_send, gather_recv, part_send, part_recv,
):
    rows, width = sources.shape
    per = rows // nc
    q = nr // nc
    nx = nc // CORES
    columns = alls.shape[1]
    blocks = columns // LANES
    own_blocks = rows // LANES
    chunks = min(nc, 4)
    group = nc // chunks
    span = rows // chunks
    log_mass = -math.log2(columns)
    scale = math.log2(math.e) / (width * entropy_weight)

    c = lax.axis_index("cluster")
    r = lax.axis_index("row")
    x, core = c // CORES, c % CORES
    k, y = r // q, r % q

    def member(mx, mcore, my):
        return (mx * CORES + mcore) * q + my

    def device(mx, mcore, my):
        return (mx * CORES + mcore, k * q + my)

    me = member(x, core, y)

    def line(d):
        return lax.rem(k + d, nc)

    barrier = pltpu.get_barrier_semaphore()
    for d in range(1, nc):
        pl.semaphore_signal(barrier, inc=1, device_id=(c, line(d) * q + y), device_id_type=MESH)
    others = []
    for dx in range(nx):
        for dcore in range(CORES):
            for dy in range(q):
                if dx or dcore or dy:
                    others.append((lax.rem(x + dx, nx), lax.rem(core + dcore, CORES), lax.rem(y + dy, q)))
    for other in others:
        pl.semaphore_signal(barrier, inc=1, device_id=device(*other), device_id_type=MESH)

    def selector(ordering):
        positions = lax.broadcasted_iota(jnp.int32, (rows, rows), 0)
        return (positions == ordering[...]).astype(jnp.float32).astype(jnp.bfloat16)

    def own_rows(t, block, owner=me):
        return alls.at[t, pl.ds(pl.multiple_of(owner * rows + block * per, per), per)]

    def into_slots(t, ordering, matrix):
        slots = jnp.dot(selector(ordering), matrix[...], preferred_element_type=jnp.float32)
        sent[t] = slots.astype(jnp.bfloat16)
        own_rows(t, 0)[...] = sent[t, pl.ds(pl.multiple_of(k * per, per), per)]

    def line_copy(t, d):
        return pltpu.make_async_remote_copy(
            src_ref=sent.at[t, pl.ds(pl.multiple_of(line(d) * per, per), per)],
            dst_ref=own_rows(t, nc - d),
            send_sem=own_send.at[t, d],
            recv_sem=own_recv.at[t, d],
            device_id=(c, line(d) * q + y),
            device_id_type=MESH,
        )

    into_slots(0, target_order, targets)
    pl.semaphore_wait(barrier, nc - 1 + nr - 1)
    for d in range(1, nc):
        line_copy(0, d).start()
    into_slots(1, source_order, sources)

    counts = [0, 0]

    def chunk_rows(t, i, owner):
        start = owner * rows + i * span
        return alls.at[t, pl.ds(pl.multiple_of(start, span), span)]

    def forward(t, i, owner, target):
        number = counts[t]
        counts[t] += 1
        owner = member(*owner)
        where = chunk_rows(t, i, owner)
        copy = pltpu.make_async_remote_copy(
            src_ref=where, dst_ref=where,
            send_sem=gather_send.at[t, number], recv_sem=gather_recv.at[t, i, owner],
            device_id=device(*target), device_id_type=MESH,
        )
        copy.start()

    def arrive(t, i, owner):
        owner = member(*owner)
        where = chunk_rows(t, i, owner)
        pltpu.make_async_remote_copy(
            src_ref=where, dst_ref=where,
            send_sem=gather_send.at[t, 0], recv_sem=gather_recv.at[t, i, owner],
            device_id=device(*others[0]), device_id_type=MESH,
        ).wait_recv()

    def along(i, first, second):
        return (first, second) if i % 2 == 0 else (second, first)

    def at(step, on=None):
        return (lax.rem(x + step[0], nx), core if on is None else on, lax.rem(y + step[1], q))

    def axes(i):
        return (nx, q) if i % 2 == 0 else (q, nx)

    here = (x, core, y)
    sibling_core = CORES - 1 - core
    sibling = (x, sibling_core, y)

    def gather_own(t):
        for i in range(chunks):
            for j in range(i * group, (i + 1) * group):
                if j > 0:
                    pltpu.make_async_remote_copy(
                        src_ref=sent.at[t, pl.ds(0, per)], dst_ref=own_rows(t, j),
                        send_sem=own_send.at[t, nc - j], recv_sem=own_recv.at[t, nc - j],
                        device_id=(c, line(j) * q + y), device_id_type=MESH,
                    ).wait_recv()
                    if t == 0:
                        line_copy(1, nc - j).start()
            first, second = axes(i)
            for step in range(1, first):
                forward(t, i, here, at(along(i, step, 0)))
            for step in range(1, second):
                forward(t, i, here, at(along(i, 0, step)))
            forward(t, i, here, sibling)

    def gather_first(t):
        for i in range(chunks):
            first, second = axes(i)
            for step in range(1, first):
                owner = at(along(i, step, 0))
                arrive(t, i, owner)
                for turn in range(1, second):
                    forward(t, i, owner, at(along(i, 0, turn)))
                forward(t, i, owner, sibling)

    def gather_second(t):
        for i in range(chunks):
            first, second = axes(i)
            for step in range(first):
                for turn in range(1, second):
                    owner = at(along(i, step, turn))
                    arrive(t, i, owner)
                    forward(t, i, owner, sibling)

    def gather_sibling(t, owner):
        for i in range(chunks):
            arrive(t, i, owner)

    diagonal = lax.broadcasted_iota(jnp.int32, (LANES, LANES), 0) == lax.broadcasted_iota(
        jnp.int32, (LANES, LANES), 1
    )

    def to_row(column):
        spread = jnp.broadcast_to(column, (LANES, LANES))
        return jnp.sum(jnp.where(diagonal, spread, 0.0), axis=0, keepdims=True)

    def to_column(row):
        spread = jnp.broadcast_to(row, (LANES, LANES))
        return jnp.sum(jnp.where(diagonal, spread, 0.0), axis=1, keepdims=True)

    def square_sums(matrix):
        widened = matrix.astype(jnp.float32)
        return jnp.sum(widened * widened, axis=1, keepdims=True)

    def shard(t, owner):
        return alls[t, pl.ds(pl.multiple_of(owner * rows, rows), rows)]

    def over_members(which, body):
        def step(index, _):
            body(member(index // q, which, lax.rem(index, q)))
            return 0

        lax.fori_loop(0, nx * q, step, 0)

    def square_panels(t, which):
        def panel(owner):
            squares = square_sums(shard(t, owner))
            for b in range(own_blocks):
                square_rows[t, pl.ds(owner * own_blocks + b, 1), :] = to_row(
                    squares[b * LANES : (b + 1) * LANES]
                )

        over_members(which, panel)

    def build(t, which):
        own = shard(t, me)
        own_squares = square_sums(own)

        def panel(owner):
            inner = lax.dot_general(
                own, shard(1 - t, owner), (((1,), (1,)), ((), ())),
                preferred_element_type=jnp.float32,
            )
            squares = jnp.concatenate(
                [square_rows[1 - t, pl.ds(owner * own_blocks + b, 1), :] for b in range(own_blocks)],
                axis=1,
            )
            cost[t, :, pl.ds(pl.multiple_of(owner * rows, rows), rows)] = scale * (
                2.0 * inner - own_squares - squares
            )

        over_members(which, panel)

    def row_pass():
        def half(h, _):
            part = pl.ds(pl.multiple_of(h * LANES, LANES), LANES)

            def scores(b):
                return cost[1, part, b * LANES : (b + 1) * LANES] + potentials[1, b : b + 1, :]

            peak = functools.reduce(jnp.maximum, (scores(b) for b in range(blocks)))
            peak = jnp.max(peak, axis=1, keepdims=True)
            total = jnp.zeros((LANES, LANES), jnp.float32)
            for b in range(blocks):
                total = total + jnp.exp2(scores(b) - peak)
            norm = peak + jnp.log2(jnp.sum(total, axis=1, keepdims=True))
            norms[1, part, :] = jnp.broadcast_to(norm, (LANES, LANES))
            return 0

        lax.fori_loop(0, own_blocks, half, 0)

    def column_pass():
        def block(b, _):
            lanes = pl.ds(pl.multiple_of(b * LANES, LANES), LANES)
            scores = cost[1, :, lanes] + (log_mass - norms[1])
            peak = jnp.max(scores, axis=0, keepdims=True)
            peaks[pl.ds(b, 1), :] = peak
            sums[pl.ds(b, 1), :] = jnp.sum(jnp.exp2(scores - peak), axis=0, keepdims=True)
            return 0

        lax.fori_loop(0, blocks, block, 0, unroll=2)
        return peaks[...] + jnp.log2(sums[...])

    def part_copy(repeat, number, owner):
        where = parts.at[repeat, owner, pl.ds(0, blocks + own_blocks)]
        return pltpu.make_async_remote_copy(
            src_ref=where,
            dst_ref=where,
            send_sem=part_send.at[repeat, number],
            recv_sem=part_recv.at[repeat, owner],
            device_id=device(*others[number]),
            device_id_type=MESH,
        )

    gather_own(0)
    gather_first(0)
    gather_second(0)
    gather_own(1)
    square_panels(0, core)
    build(1, core)
    for dx in range(nx):
        for dy in range(q):
            gather_sibling(0, at((dx, dy), sibling_core))
    square_panels(0, sibling_core)
    gather_first(1)
    build(1, sibling_core)

    potentials[1] = jnp.zeros_like(potentials[1])

    def iteration(repeat, _):
        row_pass()
        parts[repeat, me, 0:blocks, :] = column_pass()
        for b in range(own_blocks):
            parts[repeat, me, blocks + b : blocks + b + 1, :] = to_row(
                log_mass - norms[1, b * LANES : (b + 1) * LANES, :]
            )
        for number in range(len(others)):
            part_copy(repeat, number, me).start()

        @pl.when(repeat == 0)
        def _():
            gather_second(1)

        @pl.when(repeat == 1)
        def _():
            square_panels(1, core)
            build(0, core)

        @pl.when(repeat == ITERS - 1)
        def _():
            for dx in range(nx):
                for dy in range(q):
                    gather_sibling(1, at((dx, dy), sibling_core))
            square_panels(1, sibling_core)
            build(0, sibling_core)

        for number, other in enumerate(others):
            part_copy(repeat, number, member(*other)).wait_recv()
        each = [parts[repeat, m, 0:blocks, :] for m in range(nr)]
        peak = functools.reduce(jnp.maximum, each)
        column_norm = peak + jnp.log2(sum(jnp.exp2(one - peak) for one in each))
        potentials[1] = log_mass - column_norm
        sums[...] = column_norm
        return 0

    lax.fori_loop(0, ITERS, iteration, 0)

    def back_copy(t, d):
        return pltpu.make_async_remote_copy(
            src_ref=maps.at[t, pl.ds(pl.multiple_of(d * per, per), per)],
            dst_ref=back.at[t, pl.ds(pl.multiple_of(k * per, per), per)],
            send_sem=out_send.at[t, d],
            recv_sem=out_recv.at[t, d],
            device_id=(c, line(d) * q + y),
            device_id_type=MESH,
        )

    for m in range(nr):
        potentials[0, m * own_blocks : (m + 1) * own_blocks, :] = parts[
            ITERS - 1, m, blocks : blocks + own_blocks, :
        ]
    for b in range(own_blocks):
        norms[0, b * LANES : (b + 1) * LANES, :] = jnp.broadcast_to(
            to_column(sums[pl.ds(me * own_blocks + b, 1), :]), (LANES, LANES)
        )

    def mapped(t, h):
        part = pl.ds(pl.multiple_of(h * LANES, LANES), LANES)
        total = jnp.zeros((LANES, width), jnp.float32)
        step = 4 * LANES
        for start in range(0, columns, step):
            pieces = []
            for b in range(start // LANES, (start + step) // LANES):
                scores = cost[t, part, b * LANES : (b + 1) * LANES] + potentials[t, b : b + 1, :]
                pieces.append(jnp.exp2(scores - norms[t, part, :]).astype(jnp.bfloat16))
            total = total + jnp.dot(
                jnp.concatenate(pieces, axis=1),
                alls[1 - t, start : start + step, :],
                preferred_element_type=jnp.float32,
            )
        maps[t, part] = total.astype(jnp.bfloat16)
        for j in range(LANES // per):
            d = h * (LANES // per) + j

            @pl.when(d > 0)
            def _():
                back_copy(t, d).start()

    def both_maps(t, _):
        @pl.when(t == 1)
        def _():
            row_pass()

        def half(j, _):
            mapped(t, own_blocks - 1 - j)
            return 0

        lax.fori_loop(0, own_blocks, half, 0)
        back[t, pl.ds(pl.multiple_of(k * per, per), per)] = maps[t, 0:per]
        return 0

    lax.fori_loop(0, 2, both_maps, 0)

    for t in range(2):
        for d in range(1, nc):
            line_copy(t, d).wait_send()
        for number in range(counts[t]):
            pltpu.make_async_remote_copy(
                src_ref=chunk_rows(t, 0, me), dst_ref=chunk_rows(t, 0, me),
                send_sem=gather_send.at[t, number], recv_sem=gather_recv.at[t, 0, me],
                device_id=device(*others[0]), device_id_type=MESH,
            ).wait_send()
    for repeat in range(ITERS):
        for number in range(len(others)):
            part_copy(repeat, number, me).wait_send()

    def out_of_slots(t, ordering):
        for d in range(1, nc):
            back_copy(t, d).wait()
        return lax.dot_general(
            selector(ordering), back[t], (((0,), (0,)), ((), ())), preferred_element_type=jnp.float32
        ).astype(jnp.bfloat16)

    target_out[...] = out_of_slots(0, target_order)
    source_out[...] = out_of_slots(1, source_order)


def solution(mesh):
    nc, nr = mesh.shape["cluster"], mesh.shape["row"]

    def shards(sources, targets, source_order, target_order):
        rows, width = sources.shape
        columns = rows * nr
        blocks = columns // LANES
        own_blocks = rows // LANES
        nx, q = nc // CORES, nr // nc
        chunks = min(nc, 4)
        copies = chunks * max(
            a + b - 1 + (a - 1) * b + a * (b - 1) for a, b in ((nx, q), (q, nx))
        )
        vmem = pl.BlockSpec(memory_space=pltpu.VMEM)
        out = jax.ShapeDtypeStruct((rows, width), jnp.bfloat16)
        dma = pltpu.SemaphoreType.DMA
        return pl.pallas_call(
            functools.partial(kernel, nc, nr),
            out_shape=(out, out),
            in_specs=[vmem] * 4,
            out_specs=(vmem, vmem),
            scratch_shapes=[
                pltpu.VMEM((2, columns, width), jnp.bfloat16),
                pltpu.VMEM((2, rows, width), jnp.bfloat16),
                pltpu.VMEM((2, rows, width), jnp.bfloat16),
                pltpu.VMEM((2, rows, width), jnp.bfloat16),
                pltpu.VMEM((2, rows, columns), jnp.float32),
                pltpu.VMEM((2, blocks, LANES), jnp.float32),
                pltpu.VMEM((2, blocks, LANES), jnp.float32),
                pltpu.VMEM((2, rows, LANES), jnp.float32),
                pltpu.VMEM((blocks, LANES), jnp.float32),
                pltpu.VMEM((blocks, LANES), jnp.float32),
                pltpu.VMEM((ITERS, nr, blocks + 8, LANES), jnp.float32),
                dma((2, nc)), dma((2, nc)), dma((2, nc)), dma((2, nc)),
                dma((2, copies)), dma((2, chunks, nr)),
                dma((ITERS, nr)), dma((ITERS, nr)),
            ],
            compiler_params=pltpu.CompilerParams(
                collective_id=0, has_side_effects=True, vmem_limit_bytes=48 * 1024 * 1024
            ),
        )(sources, targets, source_order.reshape(1, rows), target_order.reshape(1, rows))

    return jax.shard_map(
        shards,
        mesh=mesh,
        in_specs=(
            P(("cluster", "row"), None),
            P(("cluster", "row"), None),
            P(("cluster", "row")),
            P(("cluster", "row")),
        ),
        out_specs=(P(("cluster", "row"), None), P(("cluster", "row"), None)),
        check_vma=False,
    )
```

```python
import functools
import math

import jax
import jax.numpy as jnp
from jax import lax
from jax.experimental import pallas as pl
from jax.experimental.pallas import tpu as pltpu
from jax.sharding import PartitionSpec as P

ITERS = 3
entropy_weight = 0.02
LANES = 128
CORES = 2
MESH = pl.DeviceIdType.MESH


def kernel(
    nc, nr, sources, targets, source_order, target_order, source_out, target_out,
    all_s, all_t, sent, maps, back, cost_s, cost_t, potential, source_row, peaks, sums, parts,
    out_send, out_recv, own_send, own_recv, gather_send, gather_recv, part_send, part_recv,
):
    rows, width = sources.shape
    per = rows // nc
    q = nr // nc
    nx = nc // CORES
    columns = all_s.shape[0]
    blocks = columns // LANES
    own_blocks = rows // LANES
    chunks = min(nc, 4)
    group = nc // chunks
    span = rows // chunks
    log_mass = -math.log2(columns)
    scale = math.log2(math.e) / (width * entropy_weight)

    c = lax.axis_index("cluster")
    r = lax.axis_index("row")
    x, core = c // CORES, c % CORES
    k, y = r // q, r % q
    alls = (all_t, all_s)

    def member(mx, mcore, my):
        return (mx * CORES + mcore) * q + my

    def device(mx, mcore, my):
        return (mx * CORES + mcore, k * q + my)

    me = member(x, core, y)

    def line(d):
        return lax.rem(k + d, nc)

    barrier = pltpu.get_barrier_semaphore()
    for d in range(1, nc):
        pl.semaphore_signal(barrier, inc=1, device_id=(c, line(d) * q + y), device_id_type=MESH)
    others = []
    for dx in range(nx):
        for dcore in range(CORES):
            for dy in range(q):
                if dx or dcore or dy:
                    others.append((lax.rem(x + dx, nx), lax.rem(core + dcore, CORES), lax.rem(y + dy, q)))
    for other in others:
        pl.semaphore_signal(barrier, inc=1, device_id=device(*other), device_id_type=MESH)

    def selector(ordering):
        positions = lax.broadcasted_iota(jnp.int32, (rows, rows), 0)
        return (positions == ordering[...]).astype(jnp.float32).astype(jnp.bfloat16)

    def own_rows(t, block, size):
        return alls[t].at[pl.ds(pl.multiple_of(me * rows + block * size, size), size)]

    def into_slots(t, ordering, matrix):
        slots = jnp.dot(selector(ordering), matrix[...], preferred_element_type=jnp.float32)
        sent[t] = slots.astype(jnp.bfloat16)
        own_rows(t, k, per)[...] = sent[t, pl.ds(pl.multiple_of(k * per, per), per)]

    def line_copy(t, d):
        return pltpu.make_async_remote_copy(
            src_ref=sent.at[t, pl.ds(pl.multiple_of(line(d) * per, per), per)],
            dst_ref=own_rows(t, k, per),
            send_sem=own_send.at[t, d],
            recv_sem=own_recv.at[t, d],
            device_id=(c, line(d) * q + y),
            device_id_type=MESH,
        )

    into_slots(0, target_order, targets)
    pl.semaphore_wait(barrier, nc - 1 + nr - 1)
    line_copies = []
    for t in range(2):
        if t == 1:
            into_slots(1, source_order, sources)
        for d in range(1, nc):
            copy = line_copy(t, d)
            copy.start()
            line_copies.append(copy)

    sent_copies = []
    counts = [0, 0]

    def chunk_rows(t, i, owner):
        start = owner * rows + lax.rem(k // group + i, chunks) * span
        return alls[t].at[pl.ds(pl.multiple_of(start, span), span)]

    def forward(t, i, owner, target):
        number = counts[t]
        counts[t] += 1
        owner = member(*owner)
        where = chunk_rows(t, i, owner)
        copy = pltpu.make_async_remote_copy(
            src_ref=where, dst_ref=where,
            send_sem=gather_send.at[t, number], recv_sem=gather_recv.at[t, i, owner],
            device_id=device(*target), device_id_type=MESH,
        )
        copy.start()
        sent_copies.append(copy)

    def arrive(t, i, owner):
        owner = member(*owner)
        where = chunk_rows(t, i, owner)
        pltpu.make_async_remote_copy(
            src_ref=where, dst_ref=where,
            send_sem=gather_send.at[t, 0], recv_sem=gather_recv.at[t, i, owner],
            device_id=device(*others[0]), device_id_type=MESH,
        ).wait_recv()

    def along(i, first, second):
        return (first, second) if i % 2 == 0 else (second, first)

    def at(step, on=None):
        return (lax.rem(x + step[0], nx), core if on is None else on, lax.rem(y + step[1], q))

    def axes(i):
        return (nx, q) if i % 2 == 0 else (q, nx)

    here = (x, core, y)
    sibling_core = CORES - 1 - core
    sibling = (x, sibling_core, y)

    def gather_own(t):
        if group > 1:
            for d in range(1, nc):
                line_copy(t, d).wait_recv()
        for i in range(chunks):
            if group == 1 and i > 0:
                d = nc - i
                pltpu.make_async_remote_copy(
                    src_ref=sent.at[t, pl.ds(0, per)], dst_ref=own_rows(t, line(i), per),
                    send_sem=own_send.at[t, d], recv_sem=own_recv.at[t, d],
                    device_id=(c, line(i) * q + y), device_id_type=MESH,
                ).wait_recv()
            first, second = axes(i)
            for step in range(1, first):
                forward(t, i, here, at(along(i, step, 0)))
            for step in range(1, second):
                forward(t, i, here, at(along(i, 0, step)))
            forward(t, i, here, sibling)

    def gather_first(t):
        for i in range(chunks):
            first, second = axes(i)
            for step in range(1, first):
                owner = at(along(i, step, 0))
                arrive(t, i, owner)
                for turn in range(1, second):
                    forward(t, i, owner, at(along(i, 0, turn)))
                forward(t, i, owner, sibling)

    def gather_second(t):
        for i in range(chunks):
            first, second = axes(i)
            for step in range(first):
                for turn in range(1, second):
                    owner = at(along(i, step, turn))
                    arrive(t, i, owner)
                    forward(t, i, owner, sibling)

    def gather_sibling(t, owner):
        for i in range(chunks):
            arrive(t, i, owner)

    diagonal = lax.broadcasted_iota(jnp.int32, (LANES, LANES), 0) == lax.broadcasted_iota(
        jnp.int32, (LANES, LANES), 1
    )

    def to_row(column):
        spread = jnp.broadcast_to(column, (LANES, LANES))
        return jnp.sum(jnp.where(diagonal, spread, 0.0), axis=0, keepdims=True)

    def to_column(row):
        spread = jnp.broadcast_to(row, (LANES, LANES))
        return jnp.sum(jnp.where(diagonal, spread, 0.0), axis=1, keepdims=True)

    def square_sums(matrix):
        widened = matrix.astype(jnp.float32)
        return jnp.sum(widened * widened, axis=1, keepdims=True)

    def shard(ref, owner):
        return ref[pl.ds(pl.multiple_of(owner * rows, rows), rows)]

    def build(out, own_ref, all_ref, owners):
        own = shard(own_ref, me)
        own_norms = square_sums(own)

        def panel(index, _):
            owner = owners(index)
            other = shard(all_ref, owner)
            inner = lax.dot_general(
                own, other, (((1,), (1,)), ((), ())), preferred_element_type=jnp.float32
            )
            norms = square_sums(other)
            norms = jnp.concatenate(
                [to_row(norms[b * LANES : (b + 1) * LANES]) for b in range(own_blocks)], axis=1
            )
            out[:, pl.ds(pl.multiple_of(owner * rows, rows), rows)] = scale * (
                2.0 * inner - own_norms - norms
            )
            return 0

        return panel

    def row_lse(cost, row):
        norms = []
        for h in range(own_blocks):
            part = pl.ds(h * LANES, LANES)
            peak = None
            for b in range(blocks):
                scores = cost[part, b * LANES : (b + 1) * LANES] + row[b : b + 1, :]
                peak = scores if peak is None else jnp.maximum(peak, scores)
            peak = jnp.max(peak, axis=1, keepdims=True)
            total = jnp.zeros((LANES, LANES), jnp.float32)
            for b in range(blocks):
                scores = cost[part, b * LANES : (b + 1) * LANES] + row[b : b + 1, :]
                total = total + jnp.exp2(scores - peak)
            norms.append(peak + jnp.log2(jnp.sum(total, axis=1, keepdims=True)))
        return norms

    def column_lse(cost, column):
        for b in range(blocks):
            scores = cost[:, b * LANES : (b + 1) * LANES] + column
            peak = jnp.max(scores, axis=0, keepdims=True)
            peaks[b : b + 1, :] = peak
            sums[b : b + 1, :] = jnp.sum(jnp.exp2(scores - peak), axis=0, keepdims=True)
        return peaks[...] + jnp.log2(sums[...])

    def mapped(cost, row, norms, all_ref):
        norms = jnp.concatenate(norms, axis=0)
        total = jnp.zeros((rows, width), jnp.float32)
        step = 4 * LANES
        for start in range(0, columns, step):
            pieces = []
            for b in range(start // LANES, (start + step) // LANES):
                scores = cost[:, b * LANES : (b + 1) * LANES] + row[b : b + 1, :]
                pieces.append(jnp.exp2(scores - norms).astype(jnp.bfloat16))
            total = total + jnp.dot(
                jnp.concatenate(pieces, axis=1),
                all_ref[start : start + step, :],
                preferred_element_type=jnp.float32,
            )
        return total.astype(jnp.bfloat16)

    gather_own(0)
    gather_first(0)
    gather_second(0)
    gather_own(1)
    panel = build(cost_s, all_s, all_t, lambda index: member(
        index // q, core, lax.rem(index, q)))
    lax.fori_loop(0, nx * q, panel, 0)
    for dx in range(nx):
        for dy in range(q):
            gather_sibling(0, at((dx, dy), sibling_core))
    panel = build(cost_s, all_s, all_t, lambda index: member(
        index // q, sibling_core, lax.rem(index, q)))
    lax.fori_loop(0, nx * q, panel, 0)

    potential[...] = jnp.zeros_like(potential)
    part_copies = []
    for repeat in range(ITERS):
        last = repeat == ITERS - 1
        source_potential = [log_mass - norm for norm in row_lse(cost_s, potential)]
        mine = column_lse(cost_s, jnp.concatenate(source_potential, axis=0))
        parts[repeat, me, 0:blocks, :] = mine
        used = blocks
        if last:
            for b in range(own_blocks):
                parts[repeat, me, blocks + b : blocks + b + 1, :] = to_row(source_potential[b])
            used = blocks + own_blocks
        for number, other in enumerate(others):
            copy = pltpu.make_async_remote_copy(
                src_ref=parts.at[repeat, me, pl.ds(0, used)],
                dst_ref=parts.at[repeat, me, pl.ds(0, used)],
                send_sem=part_send.at[repeat, number],
                recv_sem=part_recv.at[repeat, me],
                device_id=device(*other),
                device_id_type=MESH,
            )
            copy.start()
            part_copies.append(copy)
        if repeat == 0:
            gather_first(1)
        if repeat == 1:
            gather_second(1)
            panel = build(cost_t, all_t, all_s, lambda index: member(
                index // q, core, lax.rem(index, q)))
            lax.fori_loop(0, nx * q, panel, 0)
        if last:
            for dx in range(nx):
                for dy in range(q):
                    gather_sibling(1, at((dx, dy), sibling_core))
            panel = build(cost_t, all_t, all_s, lambda index: member(
                index // q, sibling_core, lax.rem(index, q)))
            lax.fori_loop(0, nx * q, panel, 0)
        for number, other in enumerate(others):
            owner = member(*other)
            pltpu.make_async_remote_copy(
                src_ref=parts.at[repeat, owner, pl.ds(0, used)],
                dst_ref=parts.at[repeat, owner, pl.ds(0, used)],
                send_sem=part_send.at[repeat, number],
                recv_sem=part_recv.at[repeat, owner],
                device_id=device(*other),
                device_id_type=MESH,
            ).wait_recv()
        each = [parts[repeat, m, 0:blocks, :] for m in range(nr)]
        peak = functools.reduce(jnp.maximum, each)
        column_norm = peak + jnp.log2(sum(jnp.exp2(one - peak) for one in each))
        potential[...] = log_mass - column_norm
        if last:
            sums[...] = column_norm

    def back_copy(t, d):
        return pltpu.make_async_remote_copy(
            src_ref=maps.at[t, pl.ds(pl.multiple_of(line(d) * per, per), per)],
            dst_ref=back.at[t, pl.ds(pl.multiple_of(k * per, per), per)],
            send_sem=out_send.at[t, d],
            recv_sem=out_recv.at[t, d],
            device_id=(c, line(d) * q + y),
            device_id_type=MESH,
        )

    def send_back(t):
        for d in range(1, nc):
            back_copy(t, d).start()
        own = pl.ds(pl.multiple_of(k * per, per), per)
        back[t, own] = maps[t, own]

    for m in range(nr):
        source_row[m * own_blocks : (m + 1) * own_blocks, :] = parts[
            ITERS - 1, m, blocks : blocks + own_blocks, :
        ]
    own_norm = [to_column(sums[pl.ds(me * own_blocks + b, 1), :]) for b in range(own_blocks)]
    maps[0] = mapped(cost_t, source_row, own_norm, all_s)
    send_back(0)
    maps[1] = mapped(cost_s, potential, row_lse(cost_s, potential), all_t)
    send_back(1)

    for copy in line_copies + sent_copies + part_copies:
        copy.wait_send()

    def out_of_slots(t, ordering):
        for d in range(1, nc):
            back_copy(t, d).wait()
        return lax.dot_general(
            selector(ordering), back[t], (((0,), (0,)), ((), ())), preferred_element_type=jnp.float32
        ).astype(jnp.bfloat16)

    target_out[...] = out_of_slots(0, target_order)
    source_out[...] = out_of_slots(1, source_order)


def solution(mesh):
    nc, nr = mesh.shape["cluster"], mesh.shape["row"]

    def shards(sources, targets, source_order, target_order):
        rows, width = sources.shape
        columns = rows * nr
        blocks = columns // LANES
        own_blocks = rows // LANES
        nx, q = nc // CORES, nr // nc
        chunks = min(nc, 4)
        copies = chunks * max(
            a + b - 1 + (a - 1) * b + a * (b - 1) for a, b in ((nx, q), (q, nx))
        )
        vmem = pl.BlockSpec(memory_space=pltpu.VMEM)
        out = jax.ShapeDtypeStruct((rows, width), jnp.bfloat16)
        dma = pltpu.SemaphoreType.DMA
        return pl.pallas_call(
            functools.partial(kernel, nc, nr),
            out_shape=(out, out),
            in_specs=[vmem] * 4,
            out_specs=(vmem, vmem),
            scratch_shapes=[
                pltpu.VMEM((columns, width), jnp.bfloat16),
                pltpu.VMEM((columns, width), jnp.bfloat16),
                pltpu.VMEM((2, rows, width), jnp.bfloat16),
                pltpu.VMEM((2, rows, width), jnp.bfloat16),
                pltpu.VMEM((2, rows, width), jnp.bfloat16),
                pltpu.VMEM((rows, columns), jnp.float32),
                pltpu.VMEM((rows, columns), jnp.float32),
                pltpu.VMEM((blocks, LANES), jnp.float32),
                pltpu.VMEM((blocks, LANES), jnp.float32),
                pltpu.VMEM((blocks, LANES), jnp.float32),
                pltpu.VMEM((blocks, LANES), jnp.float32),
                pltpu.VMEM((ITERS, nr, blocks + 8, LANES), jnp.float32),
                dma((2, nc)), dma((2, nc)), dma((2, nc)), dma((2, nc)),
                dma((2, copies)), dma((2, chunks, nr)),
                dma((ITERS, nr)), dma((ITERS, nr)),
            ],
            compiler_params=pltpu.CompilerParams(
                collective_id=0, has_side_effects=True, vmem_limit_bytes=48 * 1024 * 1024
            ),
        )(sources, targets, source_order.reshape(1, rows), target_order.reshape(1, rows))

    return jax.shard_map(
        shards,
        mesh=mesh,
        in_specs=(
            P(("cluster", "row"), None),
            P(("cluster", "row"), None),
            P(("cluster", "row")),
            P(("cluster", "row")),
        ),
        out_specs=(P(("cluster", "row"), None), P(("cluster", "row"), None)),
        check_vma=False,
    )
```

```python
import functools
import math

import jax
import jax.numpy as jnp
from jax import lax
from jax.experimental import pallas as pl
from jax.experimental.pallas import tpu as pltpu
from jax.sharding import PartitionSpec as P

ITERS = 3
entropy_weight = 0.02
LANES = 128
CORES = 2
MESH = pl.DeviceIdType.MESH


def kernel(
    nc, nr, sources, targets, source_order, target_order, source_out, target_out,
    all_s, all_t, sent, maps, back, cost_s, cost_t, potential, source_row, peaks, sums, parts,
    out_send, out_recv, own_send, own_recv, gather_send, gather_recv, part_send, part_recv,
):
    rows, width = sources.shape
    per = rows // nc
    q = nr // nc
    nx = nc // CORES
    columns = all_s.shape[0]
    blocks = columns // LANES
    own_blocks = rows // LANES
    chunks = min(nc, 4)
    group = nc // chunks
    span = rows // chunks
    log_mass = -math.log2(columns)
    scale = math.log2(math.e) / (width * entropy_weight)

    c = lax.axis_index("cluster")
    r = lax.axis_index("row")
    x, core = c // CORES, c % CORES
    k, y = r // q, r % q
    alls = (all_t, all_s)

    def member(mx, mcore, my):
        return (mx * CORES + mcore) * q + my

    def device(mx, mcore, my):
        return (mx * CORES + mcore, k * q + my)

    me = member(x, core, y)

    def line(d):
        return lax.rem(k + d, nc)

    barrier = pltpu.get_barrier_semaphore()
    for d in range(1, nc):
        pl.semaphore_signal(barrier, inc=1, device_id=(c, line(d) * q + y), device_id_type=MESH)
    others = []
    for dx in range(nx):
        for dcore in range(CORES):
            for dy in range(q):
                if dx or dcore or dy:
                    others.append((lax.rem(x + dx, nx), lax.rem(core + dcore, CORES), lax.rem(y + dy, q)))
    for other in others:
        pl.semaphore_signal(barrier, inc=1, device_id=device(*other), device_id_type=MESH)

    def selector(ordering):
        positions = lax.broadcasted_iota(jnp.int32, (rows, rows), 0)
        return (positions == ordering[...]).astype(jnp.float32).astype(jnp.bfloat16)

    def own_rows(t, block, size):
        return alls[t].at[pl.ds(pl.multiple_of(me * rows + block * size, size), size)]

    def into_slots(t, ordering, matrix):
        slots = jnp.dot(selector(ordering), matrix[...], preferred_element_type=jnp.float32)
        sent[t] = slots.astype(jnp.bfloat16)
        own_rows(t, k, per)[...] = sent[t, pl.ds(pl.multiple_of(k * per, per), per)]

    def line_copy(t, d):
        return pltpu.make_async_remote_copy(
            src_ref=sent.at[t, pl.ds(pl.multiple_of(line(d) * per, per), per)],
            dst_ref=own_rows(t, k, per),
            send_sem=own_send.at[t, d],
            recv_sem=own_recv.at[t, d],
            device_id=(c, line(d) * q + y),
            device_id_type=MESH,
        )

    into_slots(0, target_order, targets)
    pl.semaphore_wait(barrier, nc - 1 + nr - 1)
    line_copies = []
    for t in range(2):
        if t == 1:
            into_slots(1, source_order, sources)
        for d in range(1, nc):
            copy = line_copy(t, d)
            copy.start()
            line_copies.append(copy)

    sent_copies = []
    counts = [0, 0]

    def chunk_rows(t, i, owner):
        start = owner * rows + lax.rem(k // group + i, chunks) * span
        return alls[t].at[pl.ds(pl.multiple_of(start, span), span)]

    def forward(t, i, owner, target):
        number = counts[t]
        counts[t] += 1
        owner = member(*owner)
        where = chunk_rows(t, i, owner)
        copy = pltpu.make_async_remote_copy(
            src_ref=where, dst_ref=where,
            send_sem=gather_send.at[t, number], recv_sem=gather_recv.at[t, i, owner],
            device_id=device(*target), device_id_type=MESH,
        )
        copy.start()
        sent_copies.append(copy)

    def arrive(t, i, owner):
        owner = member(*owner)
        where = chunk_rows(t, i, owner)
        pltpu.make_async_remote_copy(
            src_ref=where, dst_ref=where,
            send_sem=gather_send.at[t, 0], recv_sem=gather_recv.at[t, i, owner],
            device_id=device(*others[0]), device_id_type=MESH,
        ).wait_recv()

    def along(i, first, second):
        return (first, second) if i % 2 == 0 else (second, first)

    def at(step, on=None):
        return (lax.rem(x + step[0], nx), core if on is None else on, lax.rem(y + step[1], q))

    def axes(i):
        return (nx, q) if i % 2 == 0 else (q, nx)

    here = (x, core, y)
    sibling_core = CORES - 1 - core
    sibling = (x, sibling_core, y)

    def gather_own(t):
        if group > 1:
            for d in range(1, nc):
                line_copy(t, d).wait_recv()
        for i in range(chunks):
            if group == 1 and i > 0:
                d = nc - i
                pltpu.make_async_remote_copy(
                    src_ref=sent.at[t, pl.ds(0, per)], dst_ref=own_rows(t, line(i), per),
                    send_sem=own_send.at[t, d], recv_sem=own_recv.at[t, d],
                    device_id=(c, line(i) * q + y), device_id_type=MESH,
                ).wait_recv()
            first, second = axes(i)
            for step in range(1, first):
                forward(t, i, here, at(along(i, step, 0)))
            for step in range(1, second):
                forward(t, i, here, at(along(i, 0, step)))
            forward(t, i, here, sibling)

    def gather_first(t):
        for i in range(chunks):
            first, second = axes(i)
            for step in range(1, first):
                owner = at(along(i, step, 0))
                arrive(t, i, owner)
                for turn in range(1, second):
                    forward(t, i, owner, at(along(i, 0, turn)))
                forward(t, i, owner, sibling)

    def gather_second(t):
        for i in range(chunks):
            first, second = axes(i)
            for step in range(first):
                for turn in range(1, second):
                    owner = at(along(i, step, turn))
                    arrive(t, i, owner)
                    forward(t, i, owner, sibling)

    def gather_sibling(t, owner):
        for i in range(chunks):
            arrive(t, i, owner)

    diagonal = lax.broadcasted_iota(jnp.int32, (LANES, LANES), 0) == lax.broadcasted_iota(
        jnp.int32, (LANES, LANES), 1
    )

    def to_row(column):
        spread = jnp.broadcast_to(column, (LANES, LANES))
        return jnp.sum(jnp.where(diagonal, spread, 0.0), axis=0, keepdims=True)

    def to_column(row):
        spread = jnp.broadcast_to(row, (LANES, LANES))
        return jnp.sum(jnp.where(diagonal, spread, 0.0), axis=1, keepdims=True)

    def square_sums(matrix):
        widened = matrix.astype(jnp.float32)
        return jnp.sum(widened * widened, axis=1, keepdims=True)

    def shard(ref, owner):
        return ref[pl.ds(pl.multiple_of(owner * rows, rows), rows)]

    def build(out, own_ref, all_ref, owners):
        own = shard(own_ref, me)
        own_norms = square_sums(own)

        def panel(index, _):
            owner = owners(index)
            other = shard(all_ref, owner)
            inner = lax.dot_general(
                own, other, (((1,), (1,)), ((), ())), preferred_element_type=jnp.float32
            )
            norms = square_sums(other)
            norms = jnp.concatenate(
                [to_row(norms[b * LANES : (b + 1) * LANES]) for b in range(own_blocks)], axis=1
            )
            out[:, pl.ds(pl.multiple_of(owner * rows, rows), rows)] = scale * (
                2.0 * inner - own_norms - norms
            )
            return 0

        return panel

    def row_lse(cost, row):
        norms = []
        for h in range(own_blocks):
            part = pl.ds(h * LANES, LANES)
            peak = None
            for b in range(blocks):
                scores = cost[part, b * LANES : (b + 1) * LANES] + row[b : b + 1, :]
                peak = scores if peak is None else jnp.maximum(peak, scores)
            peak = jnp.max(peak, axis=1, keepdims=True)
            total = jnp.zeros((LANES, LANES), jnp.float32)
            for b in range(blocks):
                scores = cost[part, b * LANES : (b + 1) * LANES] + row[b : b + 1, :]
                total = total + jnp.exp2(scores - peak)
            norms.append(peak + jnp.log2(jnp.sum(total, axis=1, keepdims=True)))
        return norms

    def column_lse(cost, column):
        for b in range(blocks):
            scores = cost[:, b * LANES : (b + 1) * LANES] + column
            peak = jnp.max(scores, axis=0, keepdims=True)
            peaks[b : b + 1, :] = peak
            sums[b : b + 1, :] = jnp.sum(jnp.exp2(scores - peak), axis=0, keepdims=True)
        return peaks[...] + jnp.log2(sums[...])

    def mapped(cost, row, norms, all_ref):
        norms = jnp.concatenate(norms, axis=0)
        total = jnp.zeros((rows, width), jnp.float32)
        step = 4 * LANES
        for start in range(0, columns, step):
            pieces = []
            for b in range(start // LANES, (start + step) // LANES):
                scores = cost[:, b * LANES : (b + 1) * LANES] + row[b : b + 1, :]
                pieces.append(jnp.exp2(scores - norms).astype(jnp.bfloat16))
            total = total + jnp.dot(
                jnp.concatenate(pieces, axis=1),
                all_ref[start : start + step, :],
                preferred_element_type=jnp.float32,
            )
        return total.astype(jnp.bfloat16)

    gather_own(0)
    gather_first(0)
    gather_second(0)
    gather_own(1)
    panel = build(cost_s, all_s, all_t, lambda index: member(
        index // q, core, lax.rem(index, q)))
    lax.fori_loop(0, nx * q, panel, 0)
    for dx in range(nx):
        for dy in range(q):
            gather_sibling(0, at((dx, dy), sibling_core))
    panel = build(cost_s, all_s, all_t, lambda index: member(
        index // q, sibling_core, lax.rem(index, q)))
    lax.fori_loop(0, nx * q, panel, 0)

    potential[...] = jnp.zeros_like(potential)
    part_copies = []
    for repeat in range(ITERS):
        last = repeat == ITERS - 1
        source_potential = [log_mass - norm for norm in row_lse(cost_s, potential)]
        mine = column_lse(cost_s, jnp.concatenate(source_potential, axis=0))
        parts[repeat, me, 0:blocks, :] = mine
        used = blocks
        if last:
            for b in range(own_blocks):
                parts[repeat, me, blocks + b : blocks + b + 1, :] = to_row(source_potential[b])
            used = blocks + own_blocks
        for number, other in enumerate(others):
            copy = pltpu.make_async_remote_copy(
                src_ref=parts.at[repeat, me, pl.ds(0, used)],
                dst_ref=parts.at[repeat, me, pl.ds(0, used)],
                send_sem=part_send.at[repeat, number],
                recv_sem=part_recv.at[repeat, me],
                device_id=device(*other),
                device_id_type=MESH,
            )
            copy.start()
            part_copies.append(copy)
        if repeat == 0:
            gather_first(1)
        if repeat == 1:
            gather_second(1)
        if last:
            panel = build(cost_t, all_t, all_s, lambda index: member(
                index // q, core, lax.rem(index, q)))
            lax.fori_loop(0, nx * q, panel, 0)
        for number, other in enumerate(others):
            owner = member(*other)
            pltpu.make_async_remote_copy(
                src_ref=parts.at[repeat, owner, pl.ds(0, used)],
                dst_ref=parts.at[repeat, owner, pl.ds(0, used)],
                send_sem=part_send.at[repeat, number],
                recv_sem=part_recv.at[repeat, owner],
                device_id=device(*other),
                device_id_type=MESH,
            ).wait_recv()
        each = [parts[repeat, m, 0:blocks, :] for m in range(nr)]
        peak = functools.reduce(jnp.maximum, each)
        column_norm = peak + jnp.log2(sum(jnp.exp2(one - peak) for one in each))
        potential[...] = log_mass - column_norm
        if last:
            sums[...] = column_norm

    def back_copy(t, d):
        return pltpu.make_async_remote_copy(
            src_ref=maps.at[t, pl.ds(pl.multiple_of(line(d) * per, per), per)],
            dst_ref=back.at[t, pl.ds(pl.multiple_of(k * per, per), per)],
            send_sem=out_send.at[t, d],
            recv_sem=out_recv.at[t, d],
            device_id=(c, line(d) * q + y),
            device_id_type=MESH,
        )

    def send_back(t):
        for d in range(1, nc):
            back_copy(t, d).start()
        own = pl.ds(pl.multiple_of(k * per, per), per)
        back[t, own] = maps[t, own]

    maps[1] = mapped(cost_s, potential, row_lse(cost_s, potential), all_t)
    send_back(1)
    for dx in range(nx):
        for dy in range(q):
            gather_sibling(1, at((dx, dy), sibling_core))
    panel = build(cost_t, all_t, all_s, lambda index: member(
        index // q, sibling_core, lax.rem(index, q)))
    lax.fori_loop(0, nx * q, panel, 0)
    for m in range(nr):
        source_row[m * own_blocks : (m + 1) * own_blocks, :] = parts[
            ITERS - 1, m, blocks : blocks + own_blocks, :
        ]
    own_norm = [to_column(sums[pl.ds(me * own_blocks + b, 1), :]) for b in range(own_blocks)]
    maps[0] = mapped(cost_t, source_row, own_norm, all_s)
    send_back(0)

    for copy in line_copies + sent_copies + part_copies:
        copy.wait_send()

    def out_of_slots(t, ordering):
        for d in range(1, nc):
            back_copy(t, d).wait()
        return lax.dot_general(
            selector(ordering), back[t], (((0,), (0,)), ((), ())), preferred_element_type=jnp.float32
        ).astype(jnp.bfloat16)

    source_out[...] = out_of_slots(1, source_order)
    target_out[...] = out_of_slots(0, target_order)


def solution(mesh):
    nc, nr = mesh.shape["cluster"], mesh.shape["row"]

    def shards(sources, targets, source_order, target_order):
        rows, width = sources.shape
        columns = rows * nr
        blocks = columns // LANES
        own_blocks = rows // LANES
        nx, q = nc // CORES, nr // nc
        chunks = min(nc, 4)
        copies = chunks * max(
            a + b - 1 + (a - 1) * b + a * (b - 1) for a, b in ((nx, q), (q, nx))
        )
        vmem = pl.BlockSpec(memory_space=pltpu.VMEM)
        out = jax.ShapeDtypeStruct((rows, width), jnp.bfloat16)
        dma = pltpu.SemaphoreType.DMA
        return pl.pallas_call(
            functools.partial(kernel, nc, nr),
            out_shape=(out, out),
            in_specs=[vmem] * 4,
            out_specs=(vmem, vmem),
            scratch_shapes=[
                pltpu.VMEM((columns, width), jnp.bfloat16),
                pltpu.VMEM((columns, width), jnp.bfloat16),
                pltpu.VMEM((2, rows, width), jnp.bfloat16),
                pltpu.VMEM((2, rows, width), jnp.bfloat16),
                pltpu.VMEM((2, rows, width), jnp.bfloat16),
                pltpu.VMEM((rows, columns), jnp.float32),
                pltpu.VMEM((rows, columns), jnp.float32),
                pltpu.VMEM((blocks, LANES), jnp.float32),
                pltpu.VMEM((blocks, LANES), jnp.float32),
                pltpu.VMEM((blocks, LANES), jnp.float32),
                pltpu.VMEM((blocks, LANES), jnp.float32),
                pltpu.VMEM((ITERS, nr, blocks + 8, LANES), jnp.float32),
                dma((2, nc)), dma((2, nc)), dma((2, nc)), dma((2, nc)),
                dma((2, copies)), dma((2, chunks, nr)),
                dma((ITERS, nr)), dma((ITERS, nr)),
            ],
            compiler_params=pltpu.CompilerParams(
                collective_id=0, has_side_effects=True, vmem_limit_bytes=48 * 1024 * 1024
            ),
        )(sources, targets, source_order.reshape(1, rows), target_order.reshape(1, rows))

    return jax.shard_map(
        shards,
        mesh=mesh,
        in_specs=(
            P(("cluster", "row"), None),
            P(("cluster", "row"), None),
            P(("cluster", "row")),
            P(("cluster", "row")),
        ),
        out_specs=(P(("cluster", "row"), None), P(("cluster", "row"), None)),
        check_vma=False,
    )
```
